512 devices in a mesh: tm: 32 (over z, core), tp: 16 (over y, x).
Axes of the slice: x: 4, y: 4, z: 16, core: 2. Of those that a mesh axis runs over, the one named last changes fastest.
Arguments:
- latents: float32 [32, 256, 64], P('tm', 'tp'), may hold values from -6 to 6
- start_latent: float32 [256, 64], P('tp'), may hold values from -6 to 6
- t_index: int32 [32], P('tm'), may hold values from 0 to 999
- dt_units: int32 [32], P('tm'), may hold values from 6 to 25
- w_time: bfloat16 [256, 9216], P(None, 'tp'), may hold values from -0.375 to 0.375
- w_in: bfloat16 [64, 3072], replicated, may hold values from -0.75 to 0.75
- w_up: bfloat16 [3072, 6144], P(None, 'tp'), may hold values from -0.109375 to 0.109375
- w_down: bfloat16 [6144, 3072], P('tp'), may hold values from -0.078125 to 0.078125
- w_out: bfloat16 [3072, 64], replicated, may hold values from -0.109375 to 0.109375
Outputs:
- new_latents: float32 [32, 256, 64], P('tm', 'tp')
- step_error: float32 [32], P('tm')
The draws below stay inside these ranges and needn't reach their ends.
All inputs are finite; a program needn't handle non-finite values.
Results may differ from the reference program's by a relative error of at most 0.0025.
Values may be sent and summed in bfloat16 or wider, within the bound.
No kernel may reach another device: no remote copies, remote signals or barrier semaphores. Data moves between devices by JAX's collectives and lax.ppermute only.
A program may use at most 64 MiB of HBM per device.

```python
import jax
import jax.numpy as jnp
from jax import lax

D = 3072
CH = 64
TEMB = 256
HID = 6144
TOK = 256
STEPS = 32


def touch_ends(drawn, key, low, top_value):
    dims = drawn.shape
    spot = [jax.random.randint(jax.random.fold_in(key, axis), (), 0, dims[axis]) for axis in range(len(dims))]
    drawn = drawn.at[tuple(spot)].set(low)
    longest = dims.index(max(dims))
    spot[longest] = (spot[longest] + 1) % dims[longest]
    return drawn.at[tuple(spot)].set(top_value)


def shard_levels(stream_key, shape, pieces, least, largest):
    level = 1.0
    for axis_at, blocks in pieces:
        steps = jax.random.uniform(jax.random.fold_in(jax.random.fold_in(stream_key, 6), axis_at), (blocks,), jnp.float32, least / len(pieces), largest / len(pieces))
        level = level * jnp.repeat(jnp.exp(steps), shape[axis_at] // blocks).reshape((-1,) + (1,) * (len(shape) - 1 - axis_at))
    return level


def noise(stream_key, shape, scale, most, shards=(), held_as=jnp.bfloat16):
    loudness = shard_levels(stream_key, shape, shards, -0.22, 0.18) if shards else 1.0
    entries = jax.random.normal(stream_key, shape, jnp.float32) * scale * loudness
    return jnp.minimum(jnp.maximum(entries, -most), most).astype(held_as)


def setup_inputs(seed: int = 0) -> dict:
    splits = jax.random.split(jax.random.key(seed), 10)
    return {
        "latents": noise(splits[0], (STEPS, TOK, CH), 1.0, 6.0, ((0, 32), (1, 16)), jnp.float32),
        "start_latent": noise(splits[1], (TOK, CH), 1.0, 6.0, ((0, 16),), jnp.float32),
        "t_index": touch_ends(jax.random.randint(splits[2], (STEPS,), 0, 1000), jax.random.fold_in(splits[2], 1), 0, 999).astype(jnp.int32),
        "dt_units": touch_ends(jax.random.randint(splits[3], (STEPS,), 6, 26), jax.random.fold_in(splits[3], 1), 6, 25).astype(jnp.int32),
        "w_time": noise(splits[4], (TEMB, 3 * D), TEMB ** -0.5, 0.375, ((1, 16),)),
        "w_in": noise(splits[5], (CH, D), CH ** -0.5, 0.75),
        "w_up": noise(splits[6], (D, HID), D ** -0.5, 0.109375, ((1, 16),)),
        "w_down": noise(splits[7], (HID, D), HID ** -0.5, 0.078125, ((0, 16),)),
        "w_out": noise(splits[8], (D, CH), D ** -0.5, 0.109375),
    }


def time_mods(step_time, w_time):
    half = w_time.shape[0] // 2
    freqs = jnp.exp(-jnp.log(10000.0) * jnp.arange(half).astype(jnp.float32) / half)
    angle = step_time.astype(jnp.float32) * freqs
    emb = jnp.concatenate([jnp.cos(angle), jnp.sin(angle)]).astype(jnp.bfloat16)
    return jnp.dot(emb[None, :], w_time, preferred_element_type=jnp.float32)[0]

def step_drift(latent, step_time, w_time, w_in, w_up, w_down, w_out):
    width = w_in.shape[1]
    mods = time_mods(step_time, w_time)
    shift = mods[:width]
    scale = mods[width:2 * width]
    gate = mods[2 * width:]
    hidden = jnp.dot(latent.astype(jnp.bfloat16), w_in, preferred_element_type=jnp.float32)
    center = hidden - lax.optimization_barrier(jnp.mean(hidden, axis=-1, keepdims=True))
    spread = lax.optimization_barrier(jnp.mean(center * center, axis=-1, keepdims=True))
    normed = (center / jnp.sqrt(spread + 1e-06) * (1.0 + scale) + shift).astype(jnp.bfloat16)
    act = jax.nn.gelu(jnp.dot(normed, w_up, preferred_element_type=jnp.float32), approximate=True).astype(jnp.bfloat16)
    mixed = hidden + gate * jnp.dot(act, w_down, preferred_element_type=jnp.float32)
    return jnp.dot(mixed, w_out.astype(jnp.float32), precision=lax.Precision.HIGHEST)

def reference(latents, start_latent, t_index, dt_units, w_time, w_in, w_up, w_down, w_out):

    def one_step(pair):
        return step_drift(pair[0], pair[1], w_time, w_in, w_up, w_down, w_out)
    drift = lax.map(one_step, (latents, t_index))
    weighted = (dt_units.astype(jnp.float32) * 0.0078125)[:, None, None] * drift
    running = jnp.cumsum(weighted, axis=0)
    before = jnp.concatenate([jnp.zeros_like(running[:1]), running[:-1]], axis=0)
    new_latents = start_latent[None] + before
    change = new_latents - latents
    step_error = lax.optimization_barrier(jnp.mean(change * change, axis=(1, 2)))
    return (new_latents, step_error)
```

```python
import jax
import jax.numpy as jnp
from jax import lax
from jax.sharding import PartitionSpec as P


def spread(value, axis):
    count = lax.axis_size(axis)
    copies = lax.optimization_barrier(jnp.broadcast_to(value[None], (count,) + value.shape))
    return lax.all_to_all(copies, axis, 0, 0, tiled=True)


def layer_norm(hidden, scale, shift):
    center = hidden - jnp.mean(hidden, axis=-1, keepdims=True)
    spread = jnp.mean(center * center, axis=-1, keepdims=True)
    return (center / jnp.sqrt(spread + 1e-06) * (1.0 + scale) + shift).astype(jnp.bfloat16)


def local(latents, start_latent, t_index, dt_units, w_time, w_in, w_up, w_down, w_out):
    width = w_in.shape[1]
    tok_rows = latents.shape[1]
    channels = latents.shape[2]
    half = w_time.shape[0] // 2
    devices = lax.axis_size("tp")
    freqs = jnp.exp(-jnp.log(10000.0) * jnp.arange(half).astype(jnp.float32) / half)
    angle = t_index.astype(jnp.float32)[:, None] * freqs[None, :]
    emb = jnp.concatenate([jnp.cos(angle), jnp.sin(angle)], axis=1).astype(jnp.bfloat16)
    mod_part = jnp.dot(emb, w_time, preferred_element_type=jnp.float32)
    sent = jnp.concatenate([mod_part.reshape(-1), latents.reshape(-1)])
    got = spread(sent, "tp")
    share = mod_part.shape[1]
    mods = got[:, :share].reshape(1, -1)
    rows = got[:, share:].reshape(devices * tok_rows, channels).astype(jnp.bfloat16)
    shift = mods[:, :width]
    scale = mods[:, width : 2 * width]
    gate = mods[:, 2 * width :]
    hidden = jnp.dot(rows, w_in, preferred_element_type=jnp.float32)
    normed = layer_norm(hidden, scale, shift)
    act = jax.nn.gelu(
        jnp.dot(normed, w_up, preferred_element_type=jnp.float32), approximate=True
    ).astype(jnp.bfloat16)
    out_full = w_out.astype(jnp.float32)
    branch = gate * jnp.dot(act, w_down, preferred_element_type=jnp.float32)
    partial = jnp.dot(branch, out_full, precision=lax.Precision.HIGHEST)
    parts = lax.all_to_all(partial.reshape(devices, tok_rows, channels), "tp", 0, 0, tiled=True)
    own = jnp.dot(latents[0].astype(jnp.bfloat16), w_in, preferred_element_type=jnp.float32)
    drift = jnp.dot(own, out_full, precision=lax.Precision.HIGHEST) + jnp.sum(parts, axis=0)
    weighted = (dt_units.astype(jnp.float32) * 0.0078125)[:, None] * drift
    steps = spread(weighted, "tm")
    earlier = lax.iota(jnp.int32, steps.shape[0]) < lax.axis_index("tm")
    before = jnp.sum(jnp.where(earlier[:, None, None], steps, 0.0), axis=0)
    new_latents = (start_latent + before)[None]
    change = new_latents - latents
    local_sum = jnp.broadcast_to(jnp.sum(change * change), (1, 128))
    total = jnp.sum(spread(local_sum, "tp")[:, 0, 0])
    step_error = (total / (tok_rows * devices * channels)).reshape(1)
    return (new_latents, step_error)


def solution(mesh):
    in_specs = (
        P("tm", "tp", None),
        P("tp", None),
        P("tm"),
        P("tm"),
        P(None, "tp"),
        P(),
        P(None, "tp"),
        P("tp", None),
        P(),
    )
    out_specs = (P("tm", "tp", None), P("tm"))
    return jax.shard_map(local, mesh=mesh, in_specs=in_specs, out_specs=out_specs, check_vma=False)
```

```python
import functools

import jax
import jax.numpy as jnp
from jax import lax
from jax.experimental import pallas as pl
from jax.experimental.pallas import tpu as pltpu
from jax.sharding import Mesh
from jax.sharding import PartitionSpec as P

LANES = 128
MODS_AT = 8
VMEM = pl.BlockSpec(memory_space=pltpu.VMEM)
SMEM = pl.BlockSpec(memory_space=pltpu.SMEM)
F32 = jnp.float32
BF16 = jnp.bfloat16


def call(body, out_shape, in_specs, name, flops=0, scratch=()):
    return pl.pallas_call(
        body,
        out_shape=out_shape,
        in_specs=in_specs,
        out_specs=jax.tree.map(lambda _: VMEM, out_shape),
        scratch_shapes=list(scratch),
        cost_estimate=pl.CostEstimate(flops=flops, bytes_accessed=1 << 20, transcendentals=0),
        compiler_params=pltpu.CompilerParams(vmem_limit_bytes=48 << 20),
        name=name,
    )


def fold(rows):
    half = rows.shape[0] // 2
    return jnp.concatenate([rows[:half], rows[half:]], axis=1)


def swap(value):
    return pltpu.roll(value, value.shape[-1] // 2, value.ndim - 1)


def left(shape):
    return lax.broadcasted_iota(jnp.int32, shape, len(shape) - 1) < shape[-1] // 2


def split(value):
    high = value.astype(BF16).astype(F32)
    return high, value - high


def prepare(place, t_index, latents, w_time, sent):
    half = w_time.shape[1] // 2
    order = lax.broadcasted_iota(jnp.int32, (16, half), 1).astype(F32)
    freqs = jnp.exp(-jnp.log(jnp.full((16, half), 10000.0, F32)) * order / half)
    angle = jnp.full((16, half), t_index[0], jnp.int32).astype(F32) * freqs
    emb = jnp.concatenate([jnp.cos(angle), jnp.sin(angle)], axis=1).astype(BF16)
    dims = (((1,), (1,)), ((), ()))
    mods = lax.dot_general(emb, w_time[...], dims, preferred_element_type=F32)[:1]
    gap = jnp.zeros((1, LANES // 2), F32)
    odd = place[0] % 2 == 1
    mods = jnp.where(odd, jnp.concatenate([gap, mods], 1), jnp.concatenate([mods, gap], 1))
    lines = mods.shape[1] // LANES
    rows = [fold(latents[0])] + [mods[:, i * LANES : (i + 1) * LANES] for i in range(lines)]
    rows.append(jnp.zeros((16 - MODS_AT - lines, LANES), F32))
    block = jnp.concatenate(rows, axis=0)
    for device in range(sent.shape[0]):
        sent[device] = block


def own_part(dt_units, latents, w_in, w_out_t, own):
    rows = latents[0].astype(BF16)
    hidden = jnp.dot(rows, w_in[...], preferred_element_type=F32)
    high, low = split(hidden)
    rest, last = split(low)
    stacked = jnp.concatenate([high, rest, last], axis=0).astype(BF16)
    dims = (((1,), (1,)), ((), ()))
    out = lax.dot_general(stacked, w_out_t[...], dims, preferred_element_type=F32)
    drift = out[:16] + out[16:32] + out[32:48]
    own[...] = fold(drift * (dt_units[0].astype(F32) * 0.0078125))


def block(place, dt_units, got, own, w_in, w_up, w_down, w_out_t, sent, hidden, normed):
    devices = got.shape[0]
    width = w_in.shape[1]
    count = width // LANES
    pairs = []
    for device in range(0, devices, 2):
        even = [got[device, MODS_AT + i : MODS_AT + i + 1, :] for i in range(5)]
        odd = [got[device + 1, MODS_AT + i : MODS_AT + i + 1, :] for i in range(5)]
        pairs += even[:4] + [even[4] + odd[0]] + odd[1:]
    shift, scale, gate = pairs[:count], pairs[count : 2 * count], pairs[2 * count :]
    dims = (((1,), (1,)), ((), ()))
    gated = w_out_t[...].astype(F32) * jnp.concatenate(gate, axis=1)
    high, low = split(gated)
    gated = jnp.concatenate([high, low], axis=0).astype(BF16)
    down = lax.dot_general(w_down[...], gated, dims, preferred_element_type=F32)
    down = down + swap(down)
    high, low = split(down)
    down = jnp.where(left(down.shape), high, low).astype(BF16)

    lat = got[:, :MODS_AT, :].reshape(devices * MODS_AT, LANES)
    lat = jnp.concatenate([lat[:, : LANES // 2], lat[:, LANES // 2 :]], axis=0).astype(BF16)
    tokens = lat.shape[0]
    step = 512
    total = jnp.zeros((tokens, LANES), F32)
    for start in range(0, width, step):
        part = jnp.dot(lat, w_in[:, start : start + step], preferred_element_type=F32)
        hidden[:, start : start + step] = part
        for at in range(0, step, LANES):
            total = total + part[:, at : at + LANES]
    mean = jnp.sum(total, axis=1, keepdims=True) / width
    total = jnp.zeros((tokens, LANES), F32)
    for start in range(0, width, LANES):
        center = hidden[:, start : start + LANES] - mean
        total = total + center * center
    spread = jnp.sum(total, axis=1, keepdims=True) / width
    inverse = 1.0 / jnp.sqrt(spread + 1e-06)
    for i in range(count):
        at = slice(i * LANES, (i + 1) * LANES)
        value = (hidden[:, at] - mean) * inverse * (1.0 + scale[i]) + shift[i]
        normed[:, at] = value.astype(BF16)
    up = jnp.dot(normed[...], w_up[...], preferred_element_type=F32)
    act = jax.nn.gelu(up, approximate=True).astype(BF16)
    part = jnp.dot(act, down, preferred_element_type=F32)
    part = part + swap(part)
    half = tokens // 2
    part = jnp.where(left((half, LANES)), part[:half], part[half:])
    part = part * (dt_units[0].astype(F32) * 0.0078125)
    part = part.reshape(devices, MODS_AT, LANES)
    mine = lax.broadcasted_iota(jnp.int32, part.shape, 0) == place[0]
    part = jnp.where(mine, part + own[...][None], part)
    sent[0] = part
    sent[1] = part


def combine(parts, sent, first):
    one = parts[0, 0]
    two = parts[1, 0]
    for device in range(1, parts.shape[1]):
        one = one + parts[0, device]
        two = two + parts[1, device]
    first[...] = one
    both = (one + two).astype(BF16)
    for device in range(sent.shape[0]):
        sent[device] = both


def finish(place, steps, first, start_latent, latents, new_latents, sent):
    before = jnp.where(place[2] == 1, first[...], 0.0)
    for z in range(steps.shape[0]):
        before = before + jnp.where(z < place[1], steps[z].astype(F32), 0.0)
    half = LANES // 2
    before = jnp.concatenate([before[:, :half], before[:, half:]], axis=0)
    value = start_latent[...] + before
    new_latents[0] = value
    change = value - latents[0]
    total = jnp.sum(change * change)
    sent[...] = jnp.full(sent.shape, total, F32)


def local(latents, start_latent, t_index, dt_units, w_time, w_in, w_up, w_down, w_out):
    zs, devices = lax.axis_size("z"), lax.axis_size("tp")
    tok_rows, channels = latents.shape[1:]
    width = w_in.shape[1]
    hid = w_up.shape[1]
    tokens = tok_rows * devices
    place = jnp.stack([lax.axis_index("tp"), lax.axis_index("z"), lax.axis_index("core")])
    w_out_t = w_out.T

    sent = call(
        prepare,
        jax.ShapeDtypeStruct((devices, 16, LANES), F32),
        [SMEM, SMEM, VMEM, VMEM],
        "prepare",
    )(place, t_index, latents, w_time.T)
    got = lax.all_to_all(sent, "tp", 0, 0, tiled=True)
    own = call(
        own_part,
        jax.ShapeDtypeStruct((MODS_AT, LANES), F32),
        [SMEM, VMEM, VMEM, VMEM],
        "own_part",
        flops=4 * tok_rows * width * channels,
    )(dt_units, latents, w_in, w_out_t)
    sent = call(
        block,
        jax.ShapeDtypeStruct((2, devices, MODS_AT, LANES), F32),
        [SMEM, SMEM] + [VMEM] * 6,
        "block",
        flops=2 * tokens * width * (hid + channels) + 2 * hid * width * channels,
        scratch=[pltpu.VMEM((tokens, width), F32), pltpu.VMEM((tokens, width), BF16)],
    )(place, dt_units, got, own, w_in, w_up, w_down, w_out_t)
    sent = sent.reshape(2 * devices, MODS_AT, LANES)
    parts = lax.all_to_all(sent, ("core", "tp"), 0, 0, tiled=True)
    parts = parts.reshape(2, devices, MODS_AT, LANES)
    sent, first = call(
        combine,
        (
            jax.ShapeDtypeStruct((zs, MODS_AT, LANES), BF16),
            jax.ShapeDtypeStruct((MODS_AT, LANES), F32),
        ),
        [VMEM],
        "combine",
    )(parts)
    steps = lax.all_to_all(sent, "z", 0, 0, tiled=True)
    new_latents, sent = call(
        finish,
        (
            jax.ShapeDtypeStruct(latents.shape, F32),
            jax.ShapeDtypeStruct((devices, 1, LANES), F32),
        ),
        [SMEM, VMEM, VMEM, VMEM, VMEM],
        "finish",
    )(place, steps, first, start_latent, latents)
    totals = lax.all_to_all(sent, "tp", 0, 0, tiled=True)
    step_error = (jnp.sum(totals[:, 0, 0]) / (tokens * channels)).reshape(1)
    return (new_latents, step_error)


def solution(mesh):
    tm, tp = (mesh.shape["tm"], mesh.shape["tp"])
    grid = Mesh(mesh.devices.reshape(tm // 2, 2, tp), ("z", "core", "tp"))
    steps = ("z", "core")
    in_specs = (
        P(steps, "tp", None),
        P("tp", None),
        P(steps),
        P(steps),
        P(None, "tp"),
        P(),
        P(None, "tp"),
        P("tp", None),
        P(),
    )
    out_specs = (P(steps, "tp", None), P(steps))
    return jax.shard_map(local, mesh=grid, in_specs=in_specs, out_specs=out_specs, check_vma=False)
```

```python
import jax
import jax.numpy as jnp
from jax import lax
from jax.experimental import pallas as pl
from jax.experimental.pallas import tpu as pltpu
from jax.sharding import Mesh
from jax.sharding import PartitionSpec as P

LANES = 128
MODS_AT = 8
SMEM = pl.BlockSpec(memory_space=pltpu.SMEM)
VMEM = pl.BlockSpec(memory_space=pltpu.VMEM)
HBM = pl.BlockSpec(memory_space=pltpu.HBM)
F32 = jnp.float32
BF16 = jnp.bfloat16


def call(body, out_shape, in_specs, name, flops=0, scratch=(), limit=16):
    return pl.pallas_call(
        body,
        out_shape=out_shape,
        in_specs=in_specs,
        out_specs=jax.tree.map(lambda _: VMEM, out_shape),
        scratch_shapes=list(scratch),
        cost_estimate=pl.CostEstimate(flops=flops, bytes_accessed=1 << 20, transcendentals=0),
        compiler_params=pltpu.CompilerParams(vmem_limit_bytes=limit << 20),
        name=name,
    )


def held(*arrays):
    return [pltpu.with_memory_space_constraint(a, pltpu.HBM) for a in arrays]


def load(pairs, sems):
    copies = [pltpu.make_async_copy(src, dst, sems.at[i]) for i, (src, dst) in enumerate(pairs)]
    for copy in copies:
        copy.start()
    return copies


def fold(rows):
    half = rows.shape[0] // 2
    return jnp.concatenate([rows[:half], rows[half:]], axis=1)


def swap(value):
    return pltpu.roll(value, value.shape[-1] // 2, value.ndim - 1)


def left(shape):
    return lax.broadcasted_iota(jnp.int32, shape, len(shape) - 1) < shape[-1] // 2


def split(value):
    high = value.astype(BF16).astype(F32)
    return high, value - high


def prepare(t_index, dt_units, latents, w_time, *refs):
    weights, (sent, factor), here = refs[:4], refs[4:6], refs[6:10]
    lat_here, w_here, sems = refs[10:]
    pairs = [(w_time, w_here), (latents, lat_here)]
    copies = load(pairs + list(zip(weights, here)), sems)
    half = w_here.shape[1] // 2
    order = lax.broadcasted_iota(jnp.int32, (16, half), 1).astype(F32)
    freqs = jnp.exp(-jnp.log(jnp.full((16, half), 10000.0, F32)) * order / half)
    angle = jnp.full((16, half), t_index[0], jnp.int32).astype(F32) * freqs
    emb = jnp.concatenate([jnp.cos(angle), jnp.sin(angle)], axis=1).astype(BF16)
    factor[...] = jnp.full(factor.shape, dt_units[0], jnp.int32).astype(F32) * 0.0078125
    copies[1].wait()
    lat = fold(lat_here[0])
    copies[0].wait()
    dims = (((1,), (1,)), ((), ()))
    mods = lax.dot_general(emb, w_here[...], dims, preferred_element_type=F32)[:1]
    gap = jnp.zeros((1, LANES // 2), F32)
    odd = lax.axis_index("tp") % 2 == 1
    mods = jnp.where(odd, jnp.concatenate([gap, mods], 1), jnp.concatenate([mods, gap], 1))
    lines = mods.shape[1] // LANES
    rows = [lat] + [mods[:, i * LANES : (i + 1) * LANES] for i in range(lines)]
    rows.append(jnp.zeros((16 - MODS_AT - lines, LANES), F32))
    block = jnp.concatenate(rows, axis=0)
    for device in range(sent.shape[0]):
        sent[device] = block
    for copy in copies[2:]:
        copy.wait()


def block(got, factor, w_in, w_out_t, w_up, w_down, sent, hidden, normed):
    devices = got.shape[0]
    width = w_in.shape[1]
    count = width // LANES
    pairs = []
    for device in range(0, devices, 2):
        even = [got[device, MODS_AT + i : MODS_AT + i + 1, :] for i in range(5)]
        odd = [got[device + 1, MODS_AT + i : MODS_AT + i + 1, :] for i in range(5)]
        pairs += even[:4] + [even[4] + odd[0]] + odd[1:]
    shift, scale, gate = pairs[:count], pairs[count : 2 * count], pairs[2 * count :]
    dims = (((1,), (1,)), ((), ()))
    gated = w_out_t[...].astype(F32) * jnp.concatenate(gate, axis=1)
    high, low = split(gated)
    gated = jnp.concatenate([high, low], axis=0).astype(BF16)
    down = lax.dot_general(w_down[...], gated, dims, preferred_element_type=F32)
    down = down + swap(down)
    high, low = split(down)
    down = jnp.where(left(down.shape), high, low).astype(BF16)

    lat = got[:, :MODS_AT, :].reshape(devices * MODS_AT, LANES)
    lat = jnp.concatenate([lat[:, : LANES // 2], lat[:, LANES // 2 :]], axis=0).astype(BF16)
    tokens = lat.shape[0]
    step = 512
    total = jnp.zeros((tokens, LANES), F32)
    for start in range(0, width, step):
        part = jnp.dot(lat, w_in[:, start : start + step], preferred_element_type=F32)
        hidden[:, start : start + step] = part
        for at in range(0, step, LANES):
            total = total + part[:, at : at + LANES]
    place = pl.multiple_of(lax.axis_index("tp") * MODS_AT, MODS_AT)
    own = [hidden[pl.ds(place + at, MODS_AT), :] for at in (0, tokens // 2)]
    high, low = split(jnp.concatenate(own, axis=0))
    rest, last = split(low)
    own = jnp.concatenate([high, rest, last], axis=0).astype(BF16)
    own = lax.dot_general(own, w_out_t[...], dims, preferred_element_type=F32)
    own = fold(own[:16] + own[16:32] + own[32:48])
    mean = jnp.sum(total, axis=1, keepdims=True) / width
    total = jnp.zeros((tokens, LANES), F32)
    for start in range(0, width, LANES):
        center = hidden[:, start : start + LANES] - mean
        total = total + center * center
    spread = jnp.sum(total, axis=1, keepdims=True) / width
    inverse = 1.0 / jnp.sqrt(spread + 1e-06)
    for i in range(count):
        at = slice(i * LANES, (i + 1) * LANES)
        value = (hidden[:, at] - mean) * inverse * (1.0 + scale[i]) + shift[i]
        normed[:, at] = value.astype(BF16)
    up = jnp.dot(normed[...], w_up[...], preferred_element_type=F32)
    act = jax.nn.gelu(up, approximate=True).astype(BF16)
    part = jnp.dot(act, down, preferred_element_type=F32)
    part = part + swap(part)
    half = tokens // 2
    part = jnp.where(left((half, LANES)), part[:half], part[half:])
    part = part.reshape(devices, MODS_AT, LANES)
    mine = lax.broadcasted_iota(jnp.int32, part.shape, 0) == lax.axis_index("tp")
    part = jnp.where(mine, part + own[None], part) * factor[...][None]
    sent[0] = part
    sent[1] = part


def combine(parts, sent, first):
    one = parts[0, 0]
    two = parts[1, 0]
    for device in range(1, parts.shape[1]):
        one = one + parts[0, device]
        two = two + parts[1, device]
    first[...] = one
    both = (one + two).astype(BF16)
    for device in range(sent.shape[0]):
        sent[device] = both


def advance(steps, first, start_latent):
    before = jnp.where(lax.axis_index("core") == 1, first[...], 0.0)
    for z in range(steps.shape[0]):
        before = before + jnp.where(z < lax.axis_index("z"), steps[z].astype(F32), 0.0)
    half = LANES // 2
    before = jnp.concatenate([before[:, :half], before[:, half:]], axis=0)
    return start_latent[...] + before


def judge(steps, first, start_latent, latents, sent):
    change = advance(steps, first, start_latent) - latents[0]
    count = change.size * sent.shape[0]
    sent[...] = jnp.full(sent.shape, jnp.sum(change * change) / count, F32)


def finish(steps, first, start_latent, new_latents):
    new_latents[0] = advance(steps, first, start_latent)


def local(latents, start_latent, t_index, dt_units, w_time, w_in, w_up, w_down, w_out):
    zs, devices = lax.axis_size("z"), lax.axis_size("tp")
    tok_rows, channels = latents.shape[1:]
    width = w_in.shape[1]
    hid = w_up.shape[1]
    tokens = tok_rows * devices
    packed = jax.ShapeDtypeStruct((MODS_AT, LANES), F32)
    w_time_t = w_time.T
    weights = (w_in, w_out.T, w_up, w_down)

    sent, factor, *here = call(
        prepare,
        [jax.ShapeDtypeStruct((devices, 16, LANES), F32), packed]
        + [jax.ShapeDtypeStruct(w.shape, BF16) for w in weights],
        [SMEM] * 2 + [HBM] * 6,
        "prepare",
        scratch=[
            pltpu.VMEM(latents.shape, F32),
            pltpu.VMEM(w_time_t.shape, BF16),
            pltpu.SemaphoreType.DMA((6,)),
        ],
    )(t_index, dt_units, *held(latents, w_time_t, *weights))
    got = lax.all_to_all(sent, "tp", 0, 0, tiled=True)
    sent = call(
        block,
        jax.ShapeDtypeStruct((2, devices, MODS_AT, LANES), F32),
        [VMEM] * 6,
        "block",
        flops=2 * tokens * width * (hid + channels) + 2 * hid * width * channels,
        scratch=[
            pltpu.VMEM((tokens, width), F32),
            pltpu.VMEM((tokens, width), BF16),
        ],
        limit=32,
    )(got, factor, *here)
    sent = sent.reshape(2 * devices, MODS_AT, LANES)
    parts = lax.all_to_all(sent, ("core", "tp"), 0, 0, tiled=True)
    parts = parts.reshape(2, devices, MODS_AT, LANES)
    sent, first = call(
        combine,
        (jax.ShapeDtypeStruct((zs, MODS_AT, LANES), BF16), packed),
        [VMEM],
        "combine",
    )(parts)
    steps = lax.all_to_all(sent, "z", 0, 0, tiled=True)
    sent = call(
        judge,
        jax.ShapeDtypeStruct((devices, 1, LANES), F32),
        [VMEM] * 4,
        "judge",
    )(steps, first, start_latent, latents)
    totals = lax.all_to_all(sent, "tp", 0, 0, tiled=True)
    new_latents = call(
        finish,
        jax.ShapeDtypeStruct(latents.shape, F32),
        [VMEM] * 3,
        "finish",
        flops=1 << 22,
    )(steps, first, start_latent)
    step_error = jnp.sum(totals[:, 0, 0]).reshape(1)
    return (new_latents, step_error)


def solution(mesh):
    tm, tp = (mesh.shape["tm"], mesh.shape["tp"])
    grid = Mesh(mesh.devices.reshape(tm // 2, 2, tp), ("z", "core", "tp"))
    steps = ("z", "core")
    in_specs = (
        P(steps, "tp", None),
        P("tp", None),
        P(steps),
        P(steps),
        P(None, "tp"),
        P(),
        P(None, "tp"),
        P("tp", None),
        P(),
    )
    out_specs = (P(steps, "tp", None), P(steps))
    return jax.shard_map(local, mesh=grid, in_specs=in_specs, out_specs=out_specs, check_vma=False)
```

```python
import math

import jax
import jax.numpy as jnp
from jax import lax
from jax.experimental import pallas as pl
from jax.experimental.pallas import tpu as pltpu
from jax.sharding import Mesh
from jax.sharding import PartitionSpec as P

LANES = 128
MODS_AT = 8
NEAR = 4
AXES = ("far", "near", "core", "y", "x")
TP = AXES[3:]
SMEM = pl.BlockSpec(memory_space=pltpu.SMEM)
VMEM = pl.BlockSpec(memory_space=pltpu.VMEM)
HBM = pl.BlockSpec(memory_space=pltpu.HBM)
F32 = jnp.float32
BF16 = jnp.bfloat16


def call(body, out_shape, in_specs, name, flops=0, scratch=(), limit=16):
    return pl.pallas_call(
        body,
        out_shape=out_shape,
        in_specs=in_specs,
        out_specs=jax.tree.map(lambda _: VMEM, out_shape),
        scratch_shapes=list(scratch),
        cost_estimate=pl.CostEstimate(flops=flops, bytes_accessed=1 << 20, transcendentals=0),
        compiler_params=pltpu.CompilerParams(vmem_limit_bytes=limit << 20),
        name=name,
    )


def held(*arrays):
    return [pltpu.with_memory_space_constraint(a, pltpu.HBM) for a in arrays]


def load(pairs, sems):
    copies = [pltpu.make_async_copy(src, dst, sems.at[i]) for i, (src, dst) in enumerate(pairs)]
    for copy in copies:
        copy.start()
    return copies


def fold(rows):
    half = rows.shape[0] // 2
    return jnp.concatenate([rows[:half], rows[half:]], axis=1)


def swap(value):
    return pltpu.roll(value, value.shape[-1] // 2, value.ndim - 1)


def left(shape):
    return lax.broadcasted_iota(jnp.int32, shape, len(shape) - 1) < shape[-1] // 2


def split(value):
    high = value.astype(BF16).astype(F32)
    return high, value - high


def prepare(t_index, dt_units, flag, latents, w_time, *refs):
    weights, (sent, factor), here = refs[:4], refs[4:6], refs[6:10]
    lat_here, w_here, sems = refs[10:]
    pairs = [(w_time, w_here), (latents, lat_here)]
    copies = load(pairs + list(zip(weights, here)), sems)
    half = w_here.shape[1] // 2
    order = lax.broadcasted_iota(jnp.int32, (16, half), 1).astype(F32)
    freqs = jnp.exp(-jnp.log(jnp.full((16, half), 10000.0, F32)) * order / half)
    angle = jnp.full((16, half), t_index[0], jnp.int32).astype(F32) * freqs
    emb = jnp.concatenate([jnp.cos(angle), jnp.sin(angle)], axis=1).astype(BF16)
    factor[...] = jnp.full(factor.shape, dt_units[0], jnp.int32).astype(F32) * 0.0078125
    copies[1].wait()
    lat = fold(lat_here[0])
    copies[0].wait()
    dims = (((1,), (1,)), ((), ()))
    mods = lax.dot_general(emb, w_here[...], dims, preferred_element_type=F32)[:1]
    gap = jnp.zeros((1, LANES // 2), F32)
    odd = lax.axis_index(TP) % 2 == 1
    mods = jnp.where(odd, jnp.concatenate([gap, mods], 1), jnp.concatenate([mods, gap], 1))
    lines = mods.shape[1] // LANES
    rows = [lat] + [mods[:, i * LANES : (i + 1) * LANES] for i in range(lines)]
    rows.append(jnp.zeros((16 - MODS_AT - lines, LANES), F32))
    block = jnp.concatenate(rows, axis=0)
    for device in range(sent.shape[0]):
        sent[device] = block
    for copy in copies[2:]:
        copy.wait()


def block(got, factor, w_in, w_out_t, w_up, w_down, sent, hidden, normed):
    devices = got.shape[0]
    width = w_in.shape[1]
    count = width // LANES
    pairs = []
    for device in range(0, devices, 2):
        even = [got[device, MODS_AT + i : MODS_AT + i + 1, :] for i in range(5)]
        odd = [got[device + 1, MODS_AT + i : MODS_AT + i + 1, :] for i in range(5)]
        pairs += even[:4] + [even[4] + odd[0]] + odd[1:]
    shift, scale, gate = pairs[:count], pairs[count : 2 * count], pairs[2 * count :]
    dims = (((1,), (1,)), ((), ()))
    gated = w_out_t[...].astype(F32) * jnp.concatenate(gate, axis=1)
    high, low = split(gated)
    gated = jnp.concatenate([high, low], axis=0).astype(BF16)
    down = lax.dot_general(w_down[...], gated, dims, preferred_element_type=F32)
    down = down + swap(down)
    high, low = split(down)
    down = jnp.where(left(down.shape), high, low).astype(BF16)

    lat = got[:, :MODS_AT, :].reshape(devices * MODS_AT, LANES)
    lat = jnp.concatenate([lat[:, : LANES // 2], lat[:, LANES // 2 :]], axis=0).astype(BF16)
    tokens = lat.shape[0]
    step = 512
    total = jnp.zeros((tokens, LANES), F32)
    for start in range(0, width, step):
        part = jnp.dot(lat, w_in[:, start : start + step], preferred_element_type=F32)
        hidden[:, start : start + step] = part
        for at in range(0, step, LANES):
            total = total + part[:, at : at + LANES]
    place = pl.multiple_of(lax.axis_index(TP) * MODS_AT, MODS_AT)
    own = [hidden[pl.ds(place + at, MODS_AT), :] for at in (0, tokens // 2)]
    high, low = split(jnp.concatenate(own, axis=0))
    rest, last = split(low)
    own = jnp.concatenate([high, rest, last], axis=0).astype(BF16)
    own = lax.dot_general(own, w_out_t[...], dims, preferred_element_type=F32)
    own = fold(own[:16] + own[16:32] + own[32:48])
    mean = jnp.sum(total, axis=1, keepdims=True) / width
    total = jnp.zeros((tokens, LANES), F32)
    for start in range(0, width, LANES):
        center = hidden[:, start : start + LANES] - mean
        total = total + center * center
    spread = jnp.sum(total, axis=1, keepdims=True) / width
    inverse = 1.0 / jnp.sqrt(spread + 1e-06)
    for i in range(count):
        at = slice(i * LANES, (i + 1) * LANES)
        value = (hidden[:, at] - mean) * inverse * (1.0 + scale[i]) + shift[i]
        normed[:, at] = value.astype(BF16)
    up = jnp.dot(normed[...], w_up[...], preferred_element_type=F32)
    act = jax.nn.gelu(up, approximate=True).astype(BF16)
    part = jnp.dot(act, down, preferred_element_type=F32)
    part = part + swap(part)
    half = tokens // 2
    part = jnp.where(left((half, LANES)), part[:half], part[half:])
    part = part.reshape(devices, MODS_AT, LANES)
    mine = lax.broadcasted_iota(jnp.int32, part.shape, 0) == lax.axis_index(TP)
    part = jnp.where(mine, part + own[None], part) * factor[...][None]
    sent[0] = part
    sent[1] = part


def combine(parts, sent, near, first):
    one = parts[0, 0]
    two = parts[1, 0]
    for device in range(1, parts.shape[1]):
        one = one + parts[0, device]
        two = two + parts[1, device]
    first[...] = one
    both = (one + two).astype(BF16)
    for device in range(sent.shape[0]):
        sent[device] = both
    for device in range(near.shape[0]):
        near[device] = both


def advance(steps, first, start_latent):
    before = jnp.where(lax.axis_index("core") == 1, first[...], 0.0)
    here = lax.axis_index(AXES[:2])
    for z in range(steps.shape[0]):
        before = before + jnp.where(z < here, steps[z].astype(F32), 0.0)
    half = LANES // 2
    before = jnp.concatenate([before[:, :half], before[:, half:]], axis=0)
    return start_latent[...] + before


def judge(steps, first, start_latent, latents, sent):
    change = advance(steps, first, start_latent) - latents[0]
    count = change.size * lax.axis_size(TP)
    sent[...] = jnp.full(sent.shape, jnp.sum(change * change) / count, F32)


def finish(steps, first, start_latent, new_latents):
    new_latents[0] = advance(steps, first, start_latent)


def local(latents, start_latent, t_index, dt_units, w_time, w_in, w_up, w_down, w_out):
    zs, devices = lax.axis_size(AXES[:2]), lax.axis_size(TP)
    tok_rows, channels = latents.shape[1:]
    width = w_in.shape[1]
    hid = w_up.shape[1]
    tokens = tok_rows * devices
    packed = jax.ShapeDtypeStruct((MODS_AT, LANES), F32)
    w_time_t = w_time.T
    weights = (w_in, w_out.T, w_up, w_down)

    early = lax.axis_index("far") == 0
    sent, factor, *here = call(
        prepare,
        [jax.ShapeDtypeStruct((devices, 16, LANES), F32), packed]
        + [jax.ShapeDtypeStruct(w.shape, BF16) for w in weights],
        [SMEM] * 3 + [HBM] * 6,
        "prepare",
        scratch=[
            pltpu.VMEM(latents.shape, F32),
            pltpu.VMEM(w_time_t.shape, BF16),
            pltpu.SemaphoreType.DMA((6,)),
        ],
    )(t_index, dt_units, early.astype(jnp.int32).reshape(1), *held(latents, w_time_t, *weights))
    got = lax.all_to_all(sent, TP, 0, 0, tiled=True)
    sent = call(
        block,
        jax.ShapeDtypeStruct((2, devices, MODS_AT, LANES), F32),
        [VMEM] * 6,
        "block",
        flops=2 * tokens * width * (hid + channels) + 2 * hid * width * channels,
        scratch=[
            pltpu.VMEM((tokens, width), F32),
            pltpu.VMEM((tokens, width), BF16),
        ],
        limit=32,
    )(got, factor, *here)
    sent = sent.reshape(2 * devices, MODS_AT, LANES)
    parts = lax.all_to_all(sent, AXES[2:], 0, 0, tiled=True)
    parts = parts.reshape(2, devices, MODS_AT, LANES)
    sent, close, first = call(
        combine,
        [jax.ShapeDtypeStruct((n, MODS_AT, LANES), BF16) for n in (zs, NEAR)] + [packed],
        [VMEM],
        "combine",
    )(parts)

    def errors(steps, *shape):
        return call(
            judge,
            jax.ShapeDtypeStruct(shape + (LANES,), F32),
            [VMEM] * 4,
            "judge",
        )(steps, first, start_latent, latents)

    def ahead(close):
        return errors(lax.all_to_all(close, "near", 0, 0, tiled=True), MODS_AT)

    def gather(part):
        part = part[:1]
        for axis in ("x", "y"):
            part = jnp.sum(lax.all_gather(part, axis), axis=0)
        return part[0, :1]

    def exchange(steps):
        totals = lax.all_to_all(errors(steps, devices, 1), TP, 0, 0, tiled=True)
        return jnp.sum(totals[:, 0, 0]).reshape(1)

    part = lax.cond(early, ahead, lambda close: first, close)
    steps = lax.all_to_all(sent, AXES[:2], 0, 0, tiled=True)
    soon = lax.cond(early, gather, lambda part: part[0, :1], part)
    step_error = lax.cond(early, lambda steps: soon, exchange, steps)
    new_latents = call(
        finish,
        jax.ShapeDtypeStruct(latents.shape, F32),
        [VMEM] * 3,
        "finish",
        flops=1 << 22,
    )(steps, first, start_latent)
    return (new_latents, step_error)


def solution(mesh):
    tm, tp = (mesh.shape["tm"], mesh.shape["tp"])
    side = math.isqrt(tp)
    grid = Mesh(mesh.devices.reshape(tm // 2 // NEAR, NEAR, 2, side, side), AXES)
    steps = AXES[:3]
    in_specs = (
        P(steps, TP, None),
        P(TP, None),
        P(steps),
        P(steps),
        P(None, TP),
        P(),
        P(None, TP),
        P(TP, None),
        P(),
    )
    out_specs = (P(steps, TP, None), P(steps))
    return jax.shard_map(local, mesh=grid, in_specs=in_specs, out_specs=out_specs, check_vma=False)
```

```python
import math

import jax
import jax.numpy as jnp
from jax import lax
from jax.experimental import pallas as pl
from jax.experimental.pallas import tpu as pltpu
from jax.sharding import Mesh
from jax.sharding import PartitionSpec as P

LANES = 128
MODS_AT = 8
NEAR = 4
AXES = ("far", "near", "core", "y", "x")
TP = AXES[3:]
SMEM = pl.BlockSpec(memory_space=pltpu.SMEM)
VMEM = pl.BlockSpec(memory_space=pltpu.VMEM)
HBM = pl.BlockSpec(memory_space=pltpu.HBM)
F32 = jnp.float32
BF16 = jnp.bfloat16


def call(body, out_shape, in_specs, name, flops=0, scratch=(), limit=16, out_specs=None):
    return pl.pallas_call(
        body,
        out_shape=out_shape,
        in_specs=in_specs,
        out_specs=out_specs or jax.tree.map(lambda _: VMEM, out_shape),
        scratch_shapes=list(scratch),
        cost_estimate=pl.CostEstimate(flops=flops, bytes_accessed=1 << 20, transcendentals=0),
        compiler_params=pltpu.CompilerParams(vmem_limit_bytes=limit << 20),
        name=name,
    )


def held(*arrays):
    return [pltpu.with_memory_space_constraint(a, pltpu.HBM) for a in arrays]


def load(pairs, sems):
    copies = [pltpu.make_async_copy(src, dst, sems.at[i]) for i, (src, dst) in enumerate(pairs)]
    for copy in copies:
        copy.start()
    return copies


def fold(rows):
    half = rows.shape[0] // 2
    return jnp.concatenate([rows[:half], rows[half:]], axis=1)


def swap(value):
    return pltpu.roll(value, value.shape[-1] // 2, value.ndim - 1)


def left(shape):
    return lax.broadcasted_iota(jnp.int32, shape, len(shape) - 1) < shape[-1] // 2


def split(value):
    high = value.astype(BF16).astype(F32)
    return high, value - high


def prepare(t_index, dt_units, flag, latents, w_time, *refs):
    sent, factor, lat_here, w_here, sems = refs
    copies = load([(w_time, w_here), (latents, lat_here)], sems)
    half = w_here.shape[1] // 2
    order = lax.broadcasted_iota(jnp.int32, (16, half), 1).astype(F32)
    freqs = jnp.exp(-jnp.log(jnp.full((16, half), 10000.0, F32)) * order / half)
    angle = jnp.full((16, half), t_index[0], jnp.int32).astype(F32) * freqs
    emb = jnp.concatenate([jnp.cos(angle), jnp.sin(angle)], axis=1).astype(BF16)
    factor[...] = jnp.full(factor.shape, dt_units[0], jnp.int32).astype(F32) * 0.0078125
    copies[1].wait()
    lat = fold(lat_here[0])
    copies[0].wait()
    dims = (((1,), (1,)), ((), ()))
    mods = lax.dot_general(emb, w_here[...], dims, preferred_element_type=F32)[:1]
    gap = jnp.zeros((1, LANES // 2), F32)
    odd = lax.axis_index(TP) % 2 == 1
    mods = jnp.where(odd, jnp.concatenate([gap, mods], 1), jnp.concatenate([mods, gap], 1))
    lines = mods.shape[1] // LANES
    rows = [lat] + [mods[:, i * LANES : (i + 1) * LANES] for i in range(lines)]
    rows.append(jnp.zeros((16 - MODS_AT - lines, LANES), F32))
    block = jnp.concatenate(rows, axis=0)
    for device in range(sent.shape[0]):
        sent[device] = block


def block(got, factor, w_in, w_out_t, w_up, w_down, sent, hidden, normed):
    devices = got.shape[0]
    width = w_in.shape[1]
    count = width // LANES
    pairs = []
    for device in range(0, devices, 2):
        even = [got[device, MODS_AT + i : MODS_AT + i + 1, :] for i in range(5)]
        odd = [got[device + 1, MODS_AT + i : MODS_AT + i + 1, :] for i in range(5)]
        pairs += even[:4] + [even[4] + odd[0]] + odd[1:]
    shift, scale, gate = pairs[:count], pairs[count : 2 * count], pairs[2 * count :]
    dims = (((1,), (1,)), ((), ()))
    gated = w_out_t[...].astype(F32) * jnp.concatenate(gate, axis=1)
    high, low = split(gated)
    gated = jnp.concatenate([high, low], axis=0).astype(BF16)
    down = lax.dot_general(w_down[...], gated, dims, preferred_element_type=F32)
    down = down + swap(down)
    high, low = split(down)
    down = jnp.where(left(down.shape), high, low).astype(BF16)

    lat = got[:, :MODS_AT, :].reshape(devices * MODS_AT, LANES)
    lat = jnp.concatenate([lat[:, : LANES // 2], lat[:, LANES // 2 :]], axis=0).astype(BF16)
    tokens = lat.shape[0]
    step = 512
    total = jnp.zeros((tokens, LANES), F32)
    for start in range(0, width, step):
        part = jnp.dot(lat, w_in[:, start : start + step], preferred_element_type=F32)
        hidden[:, start : start + step] = part
        for at in range(0, step, LANES):
            total = total + part[:, at : at + LANES]
    place = pl.multiple_of(lax.axis_index(TP) * MODS_AT, MODS_AT)
    own = [hidden[pl.ds(place + at, MODS_AT), :] for at in (0, tokens // 2)]
    high, low = split(jnp.concatenate(own, axis=0))
    rest, last = split(low)
    own = jnp.concatenate([high, rest, last], axis=0).astype(BF16)
    own = lax.dot_general(own, w_out_t[...], dims, preferred_element_type=F32)
    own = fold(own[:16] + own[16:32] + own[32:48])
    mean = jnp.sum(total, axis=1, keepdims=True) / width
    total = jnp.zeros((tokens, LANES), F32)
    for start in range(0, width, LANES):
        center = hidden[:, start : start + LANES] - mean
        total = total + center * center
    spread = jnp.sum(total, axis=1, keepdims=True) / width
    inverse = 1.0 / jnp.sqrt(spread + 1e-06)
    for i in range(count):
        at = slice(i * LANES, (i + 1) * LANES)
        value = (hidden[:, at] - mean) * inverse * (1.0 + scale[i]) + shift[i]
        normed[:, at] = value.astype(BF16)
    up = jnp.dot(normed[...], w_up[...], preferred_element_type=F32)
    act = jax.nn.gelu(up, approximate=True).astype(BF16)
    part = jnp.dot(act, down, preferred_element_type=F32)
    part = part + swap(part)
    half = tokens // 2
    part = jnp.where(left((half, LANES)), part[:half], part[half:])
    part = part.reshape(devices, MODS_AT, LANES)
    mine = lax.broadcasted_iota(jnp.int32, part.shape, 0) == lax.axis_index(TP)
    part = jnp.where(mine, part + own[None], part) * factor[...][None]
    sent[0] = part
    sent[1] = part


def combine(parts, sent, near, first):
    one = parts[0, 0]
    two = parts[1, 0]
    for device in range(1, parts.shape[1]):
        one = one + parts[0, device]
        two = two + parts[1, device]
    first[...] = one
    both = (one + two).astype(BF16)
    for device in range(sent.shape[0]):
        sent[device] = both
    for device in range(near.shape[0]):
        near[device] = both


def advance(steps, first, start_latent):
    before = jnp.where(lax.axis_index("core") == 1, first[...], 0.0)
    here = lax.axis_index(AXES[:2])
    for z in range(steps.shape[0]):
        before = before + jnp.where(z < here, steps[z].astype(F32), 0.0)
    half = LANES // 2
    before = jnp.concatenate([before[:, :half], before[:, half:]], axis=0)
    return start_latent[...] + before


def judge(steps, first, start_latent, latents, sent):
    change = advance(steps, first, start_latent) - latents[0]
    count = change.size * lax.axis_size(TP)
    sent[...] = jnp.full(sent.shape, jnp.sum(change * change) / count, F32)


def finish(parts, steps, first, start_latent, new_latents, step_error):
    new_latents[0] = advance(steps, first, start_latent)
    step_error[0] = jnp.sum(parts[...], axis=0)[0, 0]


def local(latents, start_latent, t_index, dt_units, w_time, w_in, w_up, w_down, w_out):
    zs, devices = lax.axis_size(AXES[:2]), lax.axis_size(TP)
    tok_rows, channels = latents.shape[1:]
    width = w_in.shape[1]
    hid = w_up.shape[1]
    tokens = tok_rows * devices
    packed = jax.ShapeDtypeStruct((MODS_AT, LANES), F32)
    w_time_t = w_time.T
    weights = (w_in, w_out.T, w_up, w_down)

    early = lax.axis_index("far") == 0
    sent, factor = call(
        prepare,
        [jax.ShapeDtypeStruct((devices, 16, LANES), F32), packed],
        [SMEM] * 3 + [HBM] * 2,
        "prepare",
        flops=1 << 34,
        scratch=[
            pltpu.VMEM(latents.shape, F32),
            pltpu.VMEM(w_time_t.shape, BF16),
            pltpu.SemaphoreType.DMA((2,)),
        ],
    )(t_index, dt_units, early.astype(jnp.int32).reshape(1), *held(latents, w_time_t))
    got = lax.all_to_all(sent, TP, 0, 0, tiled=True)
    sent = call(
        block,
        jax.ShapeDtypeStruct((2, devices, MODS_AT, LANES), F32),
        [VMEM] * 6,
        "block",
        flops=2 * tokens * width * (hid + channels) + 2 * hid * width * channels,
        scratch=[
            pltpu.VMEM((tokens, width), F32),
            pltpu.VMEM((tokens, width), BF16),
        ],
        limit=32,
    )(got, factor, *weights)
    sent = sent.reshape(2 * devices, MODS_AT, LANES)
    parts = lax.all_to_all(sent, AXES[2:], 0, 0, tiled=True)
    parts = parts.reshape(2, devices, MODS_AT, LANES)
    sent, close, first = call(
        combine,
        [jax.ShapeDtypeStruct((n, MODS_AT, LANES), BF16) for n in (zs, NEAR)] + [packed],
        [VMEM],
        "combine",
    )(parts)

    def errors(steps, *shape):
        return call(
            judge,
            jax.ShapeDtypeStruct(shape + (LANES,), F32),
            [VMEM] * 4,
            "judge",
        )(steps, first, start_latent, latents)

    def ahead(close):
        return errors(lax.all_to_all(close, "near", 0, 0, tiled=True), MODS_AT)

    def gather(part):
        part = jnp.sum(lax.all_gather(part[:1], "x"), axis=0)
        return lax.all_gather(part, "y")

    def close_up(parts, steps):
        return call(
            finish,
            (jax.ShapeDtypeStruct(latents.shape, F32), jax.ShapeDtypeStruct((1,), F32)),
            [VMEM] * 4,
            "finish",
            out_specs=(VMEM, SMEM),
        )(parts, steps, first, start_latent)

    def exchange(parts, steps):
        totals = lax.all_to_all(errors(steps, devices, 1), TP, 0, 0, tiled=True)
        return close_up(totals, steps)

    part = lax.cond(early, ahead, lambda close: first, close)
    steps = lax.all_to_all(sent, AXES[:2], 0, 0, tiled=True)
    soon = lax.cond(early, gather, lambda part: part[: lax.axis_size("y"), None], part)
    new_latents, step_error = lax.cond(early, close_up, exchange, soon, steps)
    return (new_latents, step_error)


def solution(mesh):
    tm, tp = (mesh.shape["tm"], mesh.shape["tp"])
    side = math.isqrt(tp)
    grid = Mesh(mesh.devices.reshape(tm // 2 // NEAR, NEAR, 2, side, side), AXES)
    steps = AXES[:3]
    in_specs = (
        P(steps, TP, None),
        P(TP, None),
        P(steps),
        P(steps),
        P(None, TP),
        P(),
        P(None, TP),
        P(TP, None),
        P(),
    )
    out_specs = (P(steps, TP, None), P(steps))
    return jax.shard_map(local, mesh=grid, in_specs=in_specs, out_specs=out_specs, check_vma=False)
```

```python
import math

import jax
import jax.numpy as jnp
from jax import lax
from jax.experimental import pallas as pl
from jax.experimental.pallas import tpu as pltpu
from jax.sharding import Mesh
from jax.sharding import PartitionSpec as P

LANES = 128
MODS_AT = 8
NEAR = 4
AXES = ("far", "near", "core", "y", "x")
TP = AXES[3:]
SMEM = pl.BlockSpec(memory_space=pltpu.SMEM)
VMEM = pl.BlockSpec(memory_space=pltpu.VMEM)
F32 = jnp.float32
BF16 = jnp.bfloat16


def call(body, out_shape, in_specs, name, flops=0, scratch=(), limit=16, out_specs=None):
    return pl.pallas_call(
        body,
        out_shape=out_shape,
        in_specs=in_specs,
        out_specs=out_specs or jax.tree.map(lambda _: VMEM, out_shape),
        scratch_shapes=list(scratch),
        cost_estimate=pl.CostEstimate(flops=flops, bytes_accessed=1 << 20, transcendentals=0),
        compiler_params=pltpu.CompilerParams(vmem_limit_bytes=limit << 20),
        name=name,
    )


def fold(rows):
    half = rows.shape[0] // 2
    return jnp.concatenate([rows[:half], rows[half:]], axis=1)


def swap(value):
    return pltpu.roll(value, value.shape[-1] // 2, value.ndim - 1)


def left(shape):
    return lax.broadcasted_iota(jnp.int32, shape, len(shape) - 1) < shape[-1] // 2


def split(value):
    high = value.astype(BF16).astype(F32)
    return high, value - high


def table(freqs):
    half = freqs.shape[1]
    order = lax.broadcasted_iota(jnp.int32, freqs.shape, 1).astype(F32)
    freqs[...] = jnp.exp(-jnp.log(jnp.full(freqs.shape, 10000.0, F32)) * order / half)


def prepare(t_index, dt_units, flag, freqs, latents, w_time, sent, factor):
    angle = jnp.full(freqs.shape, t_index[0], jnp.int32).astype(F32) * freqs[...]
    emb = jnp.concatenate([jnp.cos(angle), jnp.sin(angle)], axis=1).astype(BF16)
    factor[...] = jnp.full(factor.shape, dt_units[0], jnp.int32).astype(F32) * 0.0078125
    lat = fold(latents[0])
    dims = (((1,), (1,)), ((), ()))
    mods = lax.dot_general(emb, w_time[...], dims, preferred_element_type=F32)[:1]
    gap = jnp.zeros((1, LANES // 2), F32)
    odd = lax.axis_index(TP) % 2 == 1
    mods = jnp.where(odd, jnp.concatenate([gap, mods], 1), jnp.concatenate([mods, gap], 1))
    lines = mods.shape[1] // LANES
    rows = [lat] + [mods[:, i * LANES : (i + 1) * LANES] for i in range(lines)]
    rows.append(jnp.zeros((16 - MODS_AT - lines, LANES), F32))
    block = jnp.concatenate(rows, axis=0)
    for device in range(sent.shape[0]):
        sent[device] = block


def block(got, factor, w_in, w_out_t, w_up, w_down, sent, hidden, normed):
    devices = got.shape[0]
    width = w_in.shape[1]
    count = width // LANES
    pairs = []
    for device in range(0, devices, 2):
        even = [got[device, MODS_AT + i : MODS_AT + i + 1, :] for i in range(5)]
        odd = [got[device + 1, MODS_AT + i : MODS_AT + i + 1, :] for i in range(5)]
        pairs += even[:4] + [even[4] + odd[0]] + odd[1:]
    shift, scale, gate = pairs[:count], pairs[count : 2 * count], pairs[2 * count :]
    dims = (((1,), (1,)), ((), ()))
    gated = w_out_t[...].astype(F32) * jnp.concatenate(gate, axis=1)
    high, low = split(gated)
    gated = jnp.concatenate([high, low], axis=0).astype(BF16)
    down = lax.dot_general(w_down[...], gated, dims, preferred_element_type=F32)
    down = down + swap(down)
    high, low = split(down)
    down = jnp.where(left(down.shape), high, low).astype(BF16)

    lat = got[:, :MODS_AT, :].reshape(devices * MODS_AT, LANES)
    lat = jnp.concatenate([lat[:, : LANES // 2], lat[:, LANES // 2 :]], axis=0).astype(BF16)
    tokens = lat.shape[0]
    step = 512
    total = jnp.zeros((tokens, LANES), F32)
    for start in range(0, width, step):
        part = jnp.dot(lat, w_in[:, start : start + step], preferred_element_type=F32)
        hidden[:, start : start + step] = part
        for at in range(0, step, LANES):
            total = total + part[:, at : at + LANES]
    place = pl.multiple_of(lax.axis_index(TP) * MODS_AT, MODS_AT)
    own = [hidden[pl.ds(place + at, MODS_AT), :] for at in (0, tokens // 2)]
    high, low = split(jnp.concatenate(own, axis=0))
    rest, last = split(low)
    own = jnp.concatenate([high, rest, last], axis=0).astype(BF16)
    own = lax.dot_general(own, w_out_t[...], dims, preferred_element_type=F32)
    own = fold(own[:16] + own[16:32] + own[32:48])
    mean = jnp.sum(total, axis=1, keepdims=True) / width
    total = jnp.zeros((tokens, LANES), F32)
    for start in range(0, width, LANES):
        center = hidden[:, start : start + LANES] - mean
        total = total + center * center
    spread = jnp.sum(total, axis=1, keepdims=True) / width
    inverse = 1.0 / jnp.sqrt(spread + 1e-06)
    for i in range(count):
        at = slice(i * LANES, (i + 1) * LANES)
        value = (hidden[:, at] - mean) * inverse * (1.0 + scale[i]) + shift[i]
        normed[:, at] = value.astype(BF16)
    up = jnp.dot(normed[...], w_up[...], preferred_element_type=F32)
    act = jax.nn.gelu(up, approximate=True).astype(BF16)
    part = jnp.dot(act, down, preferred_element_type=F32)
    part = part + swap(part)
    half = tokens // 2
    part = jnp.where(left((half, LANES)), part[:half], part[half:])
    part = part.reshape(devices, MODS_AT, LANES)
    mine = lax.broadcasted_iota(jnp.int32, part.shape, 0) == lax.axis_index(TP)
    part = jnp.where(mine, part + own[None], part) * factor[...][None]
    sent[0] = part
    sent[1] = part


def combine(parts, sent, near, first):
    one = parts[0, 0]
    two = parts[1, 0]
    for device in range(1, parts.shape[1]):
        one = one + parts[0, device]
        two = two + parts[1, device]
    first[...] = one
    both = (one + two).astype(BF16)
    for device in range(sent.shape[0]):
        sent[device] = both
    for device in range(near.shape[0]):
        near[device] = both


def advance(steps, first, start_latent):
    before = jnp.where(lax.axis_index("core") == 1, first[...], 0.0)
    here = lax.axis_index(AXES[:2])
    for z in range(steps.shape[0]):
        before = before + jnp.where(z < here, steps[z].astype(F32), 0.0)
    half = LANES // 2
    before = jnp.concatenate([before[:, :half], before[:, half:]], axis=0)
    return start_latent[...] + before


def judge(steps, first, start_latent, latents, sent):
    change = advance(steps, first, start_latent) - latents[0]
    count = change.size * lax.axis_size(TP)
    sent[...] = jnp.full(sent.shape, jnp.sum(change * change) / count, F32)


def finish(parts, steps, first, start_latent, new_latents, step_error):
    new_latents[0] = advance(steps, first, start_latent)
    step_error[0] = jnp.sum(parts[...], axis=0)[0, 0]


def local(latents, start_latent, t_index, dt_units, w_time, w_in, w_up, w_down, w_out):
    zs, devices = lax.axis_size(AXES[:2]), lax.axis_size(TP)
    tok_rows, channels = latents.shape[1:]
    width = w_in.shape[1]
    hid = w_up.shape[1]
    tokens = tok_rows * devices
    packed = jax.ShapeDtypeStruct((MODS_AT, LANES), F32)
    weights = (w_in, w_out.T, w_up, w_down)

    early = lax.axis_index("far") == 0
    flag = early.astype(jnp.int32).reshape(1)
    freqs = call(
        table,
        jax.ShapeDtypeStruct((16, w_time.shape[0] // 2), F32),
        [],
        "table",
        flops=1 << 34,
    )()
    sent, factor = call(
        prepare,
        [jax.ShapeDtypeStruct((devices, 16, LANES), F32), packed],
        [SMEM] * 3 + [VMEM] * 3,
        "prepare",
        flops=1 << 34,
    )(t_index, dt_units, flag, freqs, latents, w_time.T)
    got = lax.all_to_all(sent, TP, 0, 0, tiled=True)
    sent = call(
        block,
        jax.ShapeDtypeStruct((2, devices, MODS_AT, LANES), F32),
        [VMEM] * 6,
        "block",
        flops=2 * tokens * width * (hid + channels) + 2 * hid * width * channels,
        scratch=[
            pltpu.VMEM((tokens, width), F32),
            pltpu.VMEM((tokens, width), BF16),
        ],
        limit=32,
    )(got, factor, *weights)
    sent = sent.reshape(2 * devices, MODS_AT, LANES)
    parts = lax.all_to_all(sent, AXES[2:], 0, 0, tiled=True)
    parts = parts.reshape(2, devices, MODS_AT, LANES)
    sent, close, first = call(
        combine,
        [jax.ShapeDtypeStruct((n, MODS_AT, LANES), BF16) for n in (zs, NEAR)] + [packed],
        [VMEM],
        "combine",
    )(parts)

    def errors(steps, *shape):
        return call(
            judge,
            jax.ShapeDtypeStruct(shape + (LANES,), F32),
            [VMEM] * 4,
            "judge",
        )(steps, first, start_latent, latents)

    def ahead(close):
        return errors(lax.all_to_all(close, "near", 0, 0, tiled=True), MODS_AT)

    def gather(part):
        part = jnp.sum(lax.all_gather(part[:1], "x"), axis=0)
        return lax.all_gather(part, "y")

    def close_up(parts, steps):
        return call(
            finish,
            (jax.ShapeDtypeStruct(latents.shape, F32), jax.ShapeDtypeStruct((1,), F32)),
            [VMEM] * 4,
            "finish",
            out_specs=(VMEM, SMEM),
        )(parts, steps, first, start_latent)

    def exchange(parts, steps):
        totals = lax.all_to_all(errors(steps, devices, 1), TP, 0, 0, tiled=True)
        return close_up(totals, steps)

    part = lax.cond(early, ahead, lambda close: first, close)
    steps = lax.all_to_all(sent, AXES[:2], 0, 0, tiled=True)
    soon = lax.cond(early, gather, lambda part: part[: lax.axis_size("y"), None], part)
    new_latents, step_error = lax.cond(early, close_up, exchange, soon, steps)
    return (new_latents, step_error)


def solution(mesh):
    tm, tp = (mesh.shape["tm"], mesh.shape["tp"])
    side = math.isqrt(tp)
    grid = Mesh(mesh.devices.reshape(tm // 2 // NEAR, NEAR, 2, side, side), AXES)
    steps = AXES[:3]
    in_specs = (
        P(steps, TP, None),
        P(TP, None),
        P(steps),
        P(steps),
        P(None, TP),
        P(),
        P(None, TP),
        P(TP, None),
        P(),
    )
    out_specs = (P(steps, TP, None), P(steps))
    return jax.shard_map(local, mesh=grid, in_specs=in_specs, out_specs=out_specs, check_vma=False)
```

```python
import math

import jax
import jax.numpy as jnp
from jax import lax
from jax.experimental import pallas as pl
from jax.experimental.pallas import tpu as pltpu
from jax.sharding import Mesh
from jax.sharding import PartitionSpec as P

LANES = 128
MODS_AT = 8
NEAR = 4
AXES = ("far", "near", "core", "y", "x")
TP = AXES[3:]
SMEM = pl.BlockSpec(memory_space=pltpu.SMEM)
VMEM = pl.BlockSpec(memory_space=pltpu.VMEM)
F32 = jnp.float32
BF16 = jnp.bfloat16


def call(body, out_shape, in_specs, name, flops=0, scratch=(), limit=16, out_specs=None):
    return pl.pallas_call(
        body,
        out_shape=out_shape,
        in_specs=in_specs,
        out_specs=out_specs or jax.tree.map(lambda _: VMEM, out_shape),
        scratch_shapes=list(scratch),
        cost_estimate=pl.CostEstimate(flops=flops, bytes_accessed=1 << 20, transcendentals=0),
        compiler_params=pltpu.CompilerParams(vmem_limit_bytes=limit << 20),
        name=name,
    )


def fold(rows):
    half = rows.shape[0] // 2
    return jnp.concatenate([rows[:half], rows[half:]], axis=1)


def swap(value):
    return pltpu.roll(value, value.shape[-1] // 2, value.ndim - 1)


def left(shape):
    return lax.broadcasted_iota(jnp.int32, shape, len(shape) - 1) < shape[-1] // 2


def split(value):
    high = value.astype(BF16).astype(F32)
    return high, value - high


def table(freqs):
    half = freqs.shape[1]
    order = lax.broadcasted_iota(jnp.int32, freqs.shape, 1).astype(F32)
    freqs[...] = jnp.exp(-jnp.log(jnp.full(freqs.shape, 10000.0, F32)) * order / half)


def prepare(t_index, dt_units, flag, freqs, latents, w_time, sent, factor):
    angle = jnp.full(freqs.shape, t_index[0], jnp.int32).astype(F32) * freqs[...]
    emb = jnp.concatenate([jnp.cos(angle), jnp.sin(angle)], axis=1).astype(BF16)
    factor[...] = jnp.full(factor.shape, dt_units[0], jnp.int32).astype(F32) * 0.0078125
    lat = fold(latents[0])
    dims = (((1,), (1,)), ((), ()))
    mods = lax.dot_general(emb, w_time[...], dims, preferred_element_type=F32)[:1]
    gap = jnp.zeros((1, LANES // 2), F32)
    odd = lax.axis_index(TP) % 2 == 1
    mods = jnp.where(odd, jnp.concatenate([gap, mods], 1), jnp.concatenate([mods, gap], 1))
    lines = mods.shape[1] // LANES
    rows = [lat] + [mods[:, i * LANES : (i + 1) * LANES] for i in range(lines)]
    rows.append(jnp.zeros((16 - MODS_AT - lines, LANES), F32))
    block = jnp.concatenate(rows, axis=0)
    for device in range(sent.shape[0]):
        sent[device] = block


def block(got, factor, w_in, w_out_t, w_up, w_down, sent, hidden, normed):
    devices = got.shape[0]
    width = w_in.shape[1]
    count = width // LANES
    pairs = []
    for device in range(0, devices, 2):
        even = [got[device, MODS_AT + i : MODS_AT + i + 1, :] for i in range(5)]
        odd = [got[device + 1, MODS_AT + i : MODS_AT + i + 1, :] for i in range(5)]
        pairs += even[:4] + [even[4] + odd[0]] + odd[1:]
    shift, scale, gate = pairs[:count], pairs[count : 2 * count], pairs[2 * count :]
    dims = (((1,), (1,)), ((), ()))
    gated = w_out_t[...].astype(F32) * jnp.concatenate(gate, axis=1)
    high, low = split(gated)
    gated = jnp.concatenate([high, low], axis=0).astype(BF16)
    down = lax.dot_general(w_down[...], gated, dims, preferred_element_type=F32)
    down = down + swap(down)
    high, low = split(down)
    down = jnp.where(left(down.shape), high, low).astype(BF16)

    lat = got[:, :MODS_AT, :].reshape(devices * MODS_AT, LANES)
    lat = jnp.concatenate([lat[:, : LANES // 2], lat[:, LANES // 2 :]], axis=0).astype(BF16)
    tokens = lat.shape[0]
    step = 512
    total = jnp.zeros((tokens, LANES), F32)
    for start in range(0, width, step):
        part = jnp.dot(lat, w_in[:, start : start + step], preferred_element_type=F32)
        hidden[:, start : start + step] = part
        for at in range(0, step, LANES):
            total = total + part[:, at : at + LANES]
    place = pl.multiple_of(lax.axis_index(TP) * MODS_AT, MODS_AT)
    own = [hidden[pl.ds(place + at, MODS_AT), :] for at in (0, tokens // 2)]
    high, low = split(jnp.concatenate(own, axis=0))
    rest, last = split(low)
    own = jnp.concatenate([high, rest, last], axis=0).astype(BF16)
    own = lax.dot_general(own, w_out_t[...], dims, preferred_element_type=F32)
    own = fold(own[:16] + own[16:32] + own[32:48])
    mean = jnp.sum(total, axis=1, keepdims=True) / width
    total = jnp.zeros((tokens, LANES), F32)
    for start in range(0, width, LANES):
        center = hidden[:, start : start + LANES] - mean
        total = total + center * center
    spread = jnp.sum(total, axis=1, keepdims=True) / width
    inverse = 1.0 / jnp.sqrt(spread + 1e-06)
    for i in range(count):
        at = slice(i * LANES, (i + 1) * LANES)
        value = (hidden[:, at] - mean) * inverse * (1.0 + scale[i]) + shift[i]
        normed[:, at] = value.astype(BF16)
    up = jnp.dot(normed[...], w_up[...], preferred_element_type=F32)
    act = jax.nn.gelu(up, approximate=True).astype(BF16)
    part = jnp.dot(act, down, preferred_element_type=F32)
    part = part + swap(part)
    half = tokens // 2
    part = jnp.where(left((half, LANES)), part[:half], part[half:])
    part = part.reshape(devices, MODS_AT, LANES)
    mine = lax.broadcasted_iota(jnp.int32, part.shape, 0) == lax.axis_index(TP)
    part = jnp.where(mine, part + own[None], part) * factor[...][None]
    sent[0] = part.astype(BF16)
    sent[1] = part.astype(BF16)


def combine(parts, sent, near, first):
    one = parts[0, 0].astype(F32)
    two = parts[1, 0].astype(F32)
    for device in range(1, parts.shape[1]):
        one = one + parts[0, device].astype(F32)
        two = two + parts[1, device].astype(F32)
    first[...] = one
    both = (one + two).astype(BF16)
    for device in range(sent.shape[0]):
        sent[device] = both
    for device in range(near.shape[0]):
        near[device] = both


def advance(steps, first, start_latent):
    before = jnp.where(lax.axis_index("core") == 1, first[...], 0.0)
    here = lax.axis_index(AXES[:2])
    for z in range(steps.shape[0]):
        before = before + jnp.where(z < here, steps[z].astype(F32), 0.0)
    half = LANES // 2
    before = jnp.concatenate([before[:, :half], before[:, half:]], axis=0)
    return start_latent[...] + before


def judge(steps, first, start_latent, latents, sent):
    change = advance(steps, first, start_latent) - latents[0]
    count = change.size * lax.axis_size(TP)
    sent[...] = jnp.full(sent.shape, jnp.sum(change * change) / count, F32)


def finish(parts, steps, first, start_latent, new_latents, step_error):
    new_latents[0] = advance(steps, first, start_latent)
    step_error[0] = jnp.sum(parts[...], axis=0)[0, 0]


def local(latents, start_latent, t_index, dt_units, w_time, w_in, w_up, w_down, w_out):
    zs, devices = lax.axis_size(AXES[:2]), lax.axis_size(TP)
    tok_rows, channels = latents.shape[1:]
    width = w_in.shape[1]
    hid = w_up.shape[1]
    tokens = tok_rows * devices
    packed = jax.ShapeDtypeStruct((MODS_AT, LANES), F32)
    weights = (w_in, w_out.T, w_up, w_down)

    early = lax.axis_index("far") == 0
    flag = early.astype(jnp.int32).reshape(1)
    freqs = call(
        table,
        jax.ShapeDtypeStruct((16, w_time.shape[0] // 2), F32),
        [],
        "table",
        flops=1 << 34,
    )()
    sent, factor = call(
        prepare,
        [jax.ShapeDtypeStruct((devices, 16, LANES), F32), packed],
        [SMEM] * 3 + [VMEM] * 3,
        "prepare",
        flops=1 << 34,
    )(t_index, dt_units, flag, freqs, latents, w_time.T)
    got = lax.all_to_all(sent, TP, 0, 0, tiled=True)
    sent = call(
        block,
        jax.ShapeDtypeStruct((2, devices, MODS_AT, LANES), BF16),
        [VMEM] * 6,
        "block",
        flops=2 * tokens * width * (hid + channels) + 2 * hid * width * channels,
        scratch=[
            pltpu.VMEM((tokens, width), F32),
            pltpu.VMEM((tokens, width), BF16),
        ],
        limit=32,
    )(got, factor, *weights)
    sent = sent.reshape(2 * devices, MODS_AT, LANES)
    parts = lax.all_to_all(sent, AXES[2:], 0, 0, tiled=True)
    parts = parts.reshape(2, devices, MODS_AT, LANES)
    sent, close, first = call(
        combine,
        [jax.ShapeDtypeStruct((n, MODS_AT, LANES), BF16) for n in (zs, NEAR)] + [packed],
        [VMEM],
        "combine",
    )(parts)

    def errors(steps, *shape):
        return call(
            judge,
            jax.ShapeDtypeStruct(shape + (LANES,), F32),
            [VMEM] * 4,
            "judge",
        )(steps, first, start_latent, latents)

    def ahead(close):
        return errors(lax.all_to_all(close, "near", 0, 0, tiled=True), MODS_AT)

    def gather(part):
        part = jnp.sum(lax.all_gather(part[:1], "x"), axis=0)
        return lax.all_gather(part, "y")

    def close_up(parts, steps):
        return call(
            finish,
            (jax.ShapeDtypeStruct(latents.shape, F32), jax.ShapeDtypeStruct((1,), F32)),
            [VMEM] * 4,
            "finish",
            out_specs=(VMEM, SMEM),
        )(parts, steps, first, start_latent)

    def exchange(parts, steps):
        totals = lax.all_to_all(errors(steps, devices, 1), TP, 0, 0, tiled=True)
        return close_up(totals, steps)

    part = lax.cond(early, ahead, lambda close: first, close)
    steps = lax.all_to_all(sent, AXES[:2], 0, 0, tiled=True)
    soon = lax.cond(early, gather, lambda part: part[: lax.axis_size("y"), None], part)
    new_latents, step_error = lax.cond(early, close_up, exchange, soon, steps)
    return (new_latents, step_error)


def solution(mesh):
    tm, tp = (mesh.shape["tm"], mesh.shape["tp"])
    side = math.isqrt(tp)
    grid = Mesh(mesh.devices.reshape(tm // 2 // NEAR, NEAR, 2, side, side), AXES)
    steps = AXES[:3]
    in_specs = (
        P(steps, TP, None),
        P(TP, None),
        P(steps),
        P(steps),
        P(None, TP),
        P(),
        P(None, TP),
        P(TP, None),
        P(),
    )
    out_specs = (P(steps, TP, None), P(steps))
    return jax.shard_map(local, mesh=grid, in_specs=in_specs, out_specs=out_specs, check_vma=False)
```

```python
import math

import jax
import jax.numpy as jnp
from jax import lax
from jax.experimental import pallas as pl
from jax.experimental.pallas import tpu as pltpu
from jax.sharding import Mesh
from jax.sharding import PartitionSpec as P

LANES = 128
MODS_AT = 8
NEAR = 4
AXES = ("far", "near", "core", "y", "x")
TP = AXES[3:]
SMEM = pl.BlockSpec(memory_space=pltpu.SMEM)
VMEM = pl.BlockSpec(memory_space=pltpu.VMEM)
F32 = jnp.float32
BF16 = jnp.bfloat16


def call(body, out_shape, in_specs, name, flops=0, scratch=(), limit=16, out_specs=None):
    return pl.pallas_call(
        body,
        out_shape=out_shape,
        in_specs=in_specs,
        out_specs=out_specs or jax.tree.map(lambda _: VMEM, out_shape),
        scratch_shapes=list(scratch),
        cost_estimate=pl.CostEstimate(flops=flops, bytes_accessed=1 << 20, transcendentals=0),
        compiler_params=pltpu.CompilerParams(vmem_limit_bytes=limit << 20),
        name=name,
    )


def fold(rows):
    half = rows.shape[0] // 2
    return jnp.concatenate([rows[:half], rows[half:]], axis=1)


def swap(value):
    return pltpu.roll(value, value.shape[-1] // 2, value.ndim - 1)


def left(shape):
    return lax.broadcasted_iota(jnp.int32, shape, len(shape) - 1) < shape[-1] // 2


def split(value):
    high = value.astype(BF16).astype(F32)
    return high, value - high


def table(freqs):
    half = freqs.shape[1]
    order = lax.broadcasted_iota(jnp.int32, freqs.shape, 1).astype(F32)
    freqs[...] = jnp.exp(-jnp.log(jnp.full(freqs.shape, 10000.0, F32)) * order / half)


def prepare(t_index, dt_units, flag, freqs, latents, w_time, sent, factor):
    angle = jnp.full(freqs.shape, t_index[0], jnp.int32).astype(F32) * freqs[...]
    emb = jnp.concatenate([jnp.cos(angle), jnp.sin(angle)], axis=1).astype(BF16)
    factor[...] = jnp.full(factor.shape, dt_units[0], jnp.int32).astype(F32) * 0.0078125
    lat = fold(latents[0])
    dims = (((1,), (1,)), ((), ()))
    mods = lax.dot_general(emb, w_time[...], dims, preferred_element_type=F32)[:1]
    gap = jnp.zeros((1, LANES // 2), F32)
    odd = lax.axis_index(TP) % 2 == 1
    mods = jnp.where(odd, jnp.concatenate([gap, mods], 1), jnp.concatenate([mods, gap], 1))
    lines = mods.shape[1] // LANES
    rows = [lat] + [mods[:, i * LANES : (i + 1) * LANES] for i in range(lines)]
    rows.append(jnp.zeros((16 - MODS_AT - lines, LANES), F32))
    block = jnp.concatenate(rows, axis=0)
    for device in range(sent.shape[0]):
        sent[device] = block


def block(got, factor, w_in, w_out_t, w_up, w_down, sent, hidden, normed):
    devices = got.shape[0]
    width = w_in.shape[1]
    count = width // LANES
    pairs = []
    for device in range(0, devices, 2):
        even = [got[device, MODS_AT + i : MODS_AT + i + 1, :] for i in range(5)]
        odd = [got[device + 1, MODS_AT + i : MODS_AT + i + 1, :] for i in range(5)]
        pairs += even[:4] + [even[4] + odd[0]] + odd[1:]
    shift, scale, gate = pairs[:count], pairs[count : 2 * count], pairs[2 * count :]
    dims = (((1,), (1,)), ((), ()))
    gated = w_out_t[...].astype(F32) * jnp.concatenate(gate, axis=1)
    high, low = split(gated)
    gated = jnp.concatenate([high, low], axis=0).astype(BF16)
    down = lax.dot_general(w_down[...], gated, dims, preferred_element_type=F32)
    down = down + swap(down)
    high, low = split(down)
    down = jnp.where(left(down.shape), high, low).astype(BF16)

    lat = got[:, :MODS_AT, :].reshape(devices * MODS_AT, LANES)
    lat = jnp.concatenate([lat[:, : LANES // 2], lat[:, LANES // 2 :]], axis=0).astype(BF16)
    tokens = lat.shape[0]
    step = 512
    columns = w_in[:, :LANES].astype(F32)
    for start in range(LANES, width, LANES):
        columns = columns + w_in[:, start : start + LANES].astype(F32)
    high, low = split(columns)
    rest, last = split(low)
    columns = jnp.concatenate([high, rest, last], axis=1).astype(BF16)
    total = jnp.dot(lat, columns, preferred_element_type=F32)
    total = total[:, :LANES] + (total[:, LANES : 2 * LANES] + total[:, 2 * LANES :])
    mean = jnp.sum(total, axis=1, keepdims=True) / width
    total = jnp.zeros((tokens, LANES), F32)
    for start in range(0, width, step):
        center = jnp.dot(lat, w_in[:, start : start + step], preferred_element_type=F32) - mean
        hidden[:, start : start + step] = center
        for at in range(0, step, LANES):
            total = total + center[:, at : at + LANES] * center[:, at : at + LANES]

    own = got[lax.axis_index(TP), :MODS_AT, :]
    own = jnp.concatenate([own[:, : LANES // 2], own[:, LANES // 2 :]], axis=0).astype(BF16)
    high, low = split(jnp.dot(own, w_in[...], preferred_element_type=F32))
    rest, last = split(low)
    own = jnp.concatenate([high, rest, last], axis=0).astype(BF16)
    own = lax.dot_general(own, w_out_t[...], dims, preferred_element_type=F32)
    own = fold(own[:16] + own[16:32] + own[32:48])
    spread = jnp.sum(total, axis=1, keepdims=True) / width
    inverse = 1.0 / jnp.sqrt(spread + 1e-06)
    for i in range(count):
        at = slice(i * LANES, (i + 1) * LANES)
        value = hidden[:, at] * inverse * (1.0 + scale[i]) + shift[i]
        normed[:, at] = value.astype(BF16)
    up = jnp.dot(normed[...], w_up[...], preferred_element_type=F32)
    act = jax.nn.gelu(up, approximate=True).astype(BF16)
    part = jnp.dot(act, down, preferred_element_type=F32)
    part = part + swap(part)
    half = tokens // 2
    part = jnp.where(left((half, LANES)), part[:half], part[half:])
    part = part.reshape(devices, MODS_AT, LANES)
    mine = lax.broadcasted_iota(jnp.int32, part.shape, 0) == lax.axis_index(TP)
    part = jnp.where(mine, part + own[None], part) * factor[...][None]
    sent[0] = part.astype(BF16)
    sent[1] = part.astype(BF16)


def combine(parts, sent, near, first):
    one = parts[0, 0].astype(F32)
    two = parts[1, 0].astype(F32)
    for device in range(1, parts.shape[1]):
        one = one + parts[0, device].astype(F32)
        two = two + parts[1, device].astype(F32)
    first[...] = one
    both = (one + two).astype(BF16)
    for device in range(sent.shape[0]):
        sent[device] = both
    for device in range(near.shape[0]):
        near[device] = both


def before(steps, first):
    total = jnp.where(lax.axis_index("core") == 1, first[...], 0.0)
    here = lax.axis_index(AXES[:2])
    for z in range(steps.shape[0]):
        total = total + jnp.where(z < here, steps[z].astype(F32), 0.0)
    return total


def judge(steps, first, start_latent, latents, sent):
    change = fold(start_latent[...] - latents[0]) + before(steps, first)
    count = change.size * lax.axis_size(TP)
    part = jnp.sum(change * change, axis=0, keepdims=True) / count
    sent[...] = jnp.broadcast_to(part, sent.shape)


def finish(parts, steps, first, start_latent, new_latents, step_error):
    half = LANES // 2
    change = before(steps, first)
    change = jnp.concatenate([change[:, :half], change[:, half:]], axis=0)
    new_latents[0] = start_latent[...] + change
    step_error[0] = jnp.sum(parts[...])


def local(latents, start_latent, t_index, dt_units, w_time, w_in, w_up, w_down, w_out):
    zs, devices = lax.axis_size(AXES[:2]), lax.axis_size(TP)
    tok_rows, channels = latents.shape[1:]
    width = w_in.shape[1]
    hid = w_up.shape[1]
    tokens = tok_rows * devices
    packed = jax.ShapeDtypeStruct((MODS_AT, LANES), F32)
    weights = (w_in, w_out.T, w_up, w_down)

    early = lax.axis_index("far") == 0
    flag = early.astype(jnp.int32).reshape(1)
    freqs = call(
        table,
        jax.ShapeDtypeStruct((16, w_time.shape[0] // 2), F32),
        [],
        "table",
        flops=1 << 34,
    )()
    sent, factor = call(
        prepare,
        [jax.ShapeDtypeStruct((devices, 16, LANES), F32), packed],
        [SMEM] * 3 + [VMEM] * 3,
        "prepare",
        flops=1 << 34,
    )(t_index, dt_units, flag, freqs, latents, w_time.T)
    got = lax.all_to_all(sent, TP, 0, 0, tiled=True)
    sent = call(
        block,
        jax.ShapeDtypeStruct((2, devices, MODS_AT, LANES), BF16),
        [VMEM] * 6,
        "block",
        flops=2 * tokens * width * (hid + channels) + 2 * hid * width * channels,
        scratch=[
            pltpu.VMEM((tokens, width), F32),
            pltpu.VMEM((tokens, width), BF16),
        ],
        limit=32,
    )(got, factor, *weights)
    sent = sent.reshape(2 * devices, MODS_AT, LANES)
    parts = lax.all_to_all(sent, AXES[2:], 0, 0, tiled=True)
    parts = parts.reshape(2, devices, MODS_AT, LANES)
    sent, close, first = call(
        combine,
        [jax.ShapeDtypeStruct((n, MODS_AT, LANES), BF16) for n in (zs, NEAR)] + [packed],
        [VMEM],
        "combine",
    )(parts)

    def errors(steps, *shape):
        return call(
            judge,
            jax.ShapeDtypeStruct(shape + (LANES,), F32),
            [VMEM] * 4,
            "judge",
        )(steps, first, start_latent, latents)

    def ahead(close):
        return errors(lax.all_to_all(close, "near", 0, 0, tiled=True), MODS_AT)

    def gather(part):
        part = jnp.sum(lax.all_gather(part[:1], "x"), axis=0)
        return lax.all_gather(part, "y")

    def close_up(parts, steps):
        return call(
            finish,
            (jax.ShapeDtypeStruct(latents.shape, F32), jax.ShapeDtypeStruct((1,), F32)),
            [VMEM] * 4,
            "finish",
            out_specs=(VMEM, SMEM),
        )(parts, steps, first, start_latent)

    def exchange(parts, steps):
        totals = lax.all_to_all(errors(steps, devices, 1), TP, 0, 0, tiled=True)
        return close_up(totals, steps)

    part = lax.cond(early, ahead, lambda close: first, close)
    steps = lax.all_to_all(sent, AXES[:2], 0, 0, tiled=True)
    soon = lax.cond(early, gather, lambda part: part[: lax.axis_size("y"), None], part)
    new_latents, step_error = lax.cond(early, close_up, exchange, soon, steps)
    return (new_latents, step_error)


def solution(mesh):
    tm, tp = (mesh.shape["tm"], mesh.shape["tp"])
    side = math.isqrt(tp)
    grid = Mesh(mesh.devices.reshape(tm // 2 // NEAR, NEAR, 2, side, side), AXES)
    steps = AXES[:3]
    in_specs = (
        P(steps, TP, None),
        P(TP, None),
        P(steps),
        P(steps),
        P(None, TP),
        P(),
        P(None, TP),
        P(TP, None),
        P(),
    )
    out_specs = (P(steps, TP, None), P(steps))
    return jax.shard_map(local, mesh=grid, in_specs=in_specs, out_specs=out_specs, check_vma=False)
```

```python
import math

import jax
import jax.numpy as jnp
from jax import lax
from jax.experimental import pallas as pl
from jax.experimental.pallas import tpu as pltpu
from jax.sharding import Mesh
from jax.sharding import PartitionSpec as P

LANES = 128
MODS_AT = 8
NEAR = 4
AXES = ("far", "near", "core", "y", "x")
TP = AXES[3:]
SMEM = pl.BlockSpec(memory_space=pltpu.SMEM)
VMEM = pl.BlockSpec(memory_space=pltpu.VMEM)
F32 = jnp.float32
BF16 = jnp.bfloat16


def call(body, out_shape, in_specs, name, flops=0, scratch=(), limit=16, out_specs=None):
    return pl.pallas_call(
        body,
        out_shape=out_shape,
        in_specs=in_specs,
        out_specs=out_specs or jax.tree.map(lambda _: VMEM, out_shape),
        scratch_shapes=list(scratch),
        cost_estimate=pl.CostEstimate(flops=flops, bytes_accessed=1 << 20, transcendentals=0),
        compiler_params=pltpu.CompilerParams(vmem_limit_bytes=limit << 20),
        name=name,
    )


def fold(rows):
    half = rows.shape[0] // 2
    return jnp.concatenate([rows[:half], rows[half:]], axis=1)


def swap(value):
    return pltpu.roll(value, value.shape[-1] // 2, value.ndim - 1)


def left(shape):
    return lax.broadcasted_iota(jnp.int32, shape, len(shape) - 1) < shape[-1] // 2


def split(value):
    high = value.astype(BF16).astype(F32)
    return high, value - high


def table(freqs, early):
    early[0] = (lax.axis_index("far") == 0).astype(jnp.int32)
    half = freqs.shape[1]
    order = lax.broadcasted_iota(jnp.int32, freqs.shape, 1).astype(F32)
    freqs[...] = jnp.exp(-jnp.log(jnp.full(freqs.shape, 10000.0, F32)) * order / half)


def prepare(t_index, dt_units, flag, freqs, latents, w_time, sent, factor):
    angle = jnp.full(freqs.shape, t_index[0], jnp.int32).astype(F32) * freqs[...]
    emb = jnp.concatenate([jnp.cos(angle), jnp.sin(angle)], axis=1).astype(BF16)
    factor[...] = jnp.full(factor.shape, dt_units[0], jnp.int32).astype(F32) * 0.0078125
    lat = fold(latents[0])
    dims = (((1,), (1,)), ((), ()))
    mods = lax.dot_general(emb, w_time[...], dims, preferred_element_type=F32)[:1]
    gap = jnp.zeros((1, LANES // 2), F32)
    odd = lax.axis_index(TP) % 2 == 1
    mods = jnp.where(odd, jnp.concatenate([gap, mods], 1), jnp.concatenate([mods, gap], 1))
    lines = mods.shape[1] // LANES
    rows = [lat] + [mods[:, i * LANES : (i + 1) * LANES] for i in range(lines)]
    rows.append(jnp.zeros((16 - MODS_AT - lines, LANES), F32))
    block = jnp.concatenate(rows, axis=0)
    for device in range(sent.shape[0]):
        sent[device] = block


def block(got, factor, w_in, w_out_t, w_up, w_down, sent, hidden, normed):
    devices = got.shape[0]
    width = w_in.shape[1]
    count = width // LANES
    pairs = []
    for device in range(0, devices, 2):
        even = [got[device, MODS_AT + i : MODS_AT + i + 1, :] for i in range(5)]
        odd = [got[device + 1, MODS_AT + i : MODS_AT + i + 1, :] for i in range(5)]
        pairs += even[:4] + [even[4] + odd[0]] + odd[1:]
    shift, scale, gate = pairs[:count], pairs[count : 2 * count], pairs[2 * count :]
    dims = (((1,), (1,)), ((), ()))
    gated = w_out_t[...].astype(F32) * jnp.concatenate(gate, axis=1)
    high, low = split(gated)
    gated = jnp.concatenate([high, low], axis=0).astype(BF16)
    down = lax.dot_general(w_down[...], gated, dims, preferred_element_type=F32)
    down = down + swap(down)
    high, low = split(down)
    down = jnp.where(left(down.shape), high, low).astype(BF16)

    lat = got[:, :MODS_AT, :].reshape(devices * MODS_AT, LANES)
    lat = jnp.concatenate([lat[:, : LANES // 2], lat[:, LANES // 2 :]], axis=0).astype(BF16)
    tokens = lat.shape[0]
    step = 512
    columns = w_in[:, :LANES].astype(F32)
    for start in range(LANES, width, LANES):
        columns = columns + w_in[:, start : start + LANES].astype(F32)
    high, low = split(columns)
    rest, last = split(low)
    columns = jnp.concatenate([high, rest, last], axis=1).astype(BF16)
    total = jnp.dot(lat, columns, preferred_element_type=F32)
    total = total[:, :LANES] + (total[:, LANES : 2 * LANES] + total[:, 2 * LANES :])
    mean = jnp.sum(total, axis=1, keepdims=True) / width
    total = jnp.zeros((tokens, LANES), F32)
    for start in range(0, width, step):
        center = jnp.dot(lat, w_in[:, start : start + step], preferred_element_type=F32) - mean
        hidden[:, start : start + step] = center
        for at in range(0, step, LANES):
            total = total + center[:, at : at + LANES] * center[:, at : at + LANES]

    own = got[lax.axis_index(TP), :MODS_AT, :]
    own = jnp.concatenate([own[:, : LANES // 2], own[:, LANES // 2 :]], axis=0).astype(BF16)
    high, low = split(jnp.dot(own, w_in[...], preferred_element_type=F32))
    rest, last = split(low)
    own = jnp.concatenate([high, rest, last], axis=0).astype(BF16)
    own = lax.dot_general(own, w_out_t[...], dims, preferred_element_type=F32)
    own = fold(own[:16] + own[16:32] + own[32:48])
    spread = jnp.sum(total, axis=1, keepdims=True) / width
    inverse = 1.0 / jnp.sqrt(spread + 1e-06)
    for i in range(count):
        at = slice(i * LANES, (i + 1) * LANES)
        value = hidden[:, at] * inverse * (1.0 + scale[i]) + shift[i]
        normed[:, at] = value.astype(BF16)
    up = jnp.dot(normed[...], w_up[...], preferred_element_type=F32)
    act = jax.nn.gelu(up, approximate=True).astype(BF16)
    part = jnp.dot(act, down, preferred_element_type=F32)
    part = part + swap(part)
    half = tokens // 2
    part = jnp.where(left((half, LANES)), part[:half], part[half:])
    part = part.reshape(devices, MODS_AT, LANES)
    mine = lax.broadcasted_iota(jnp.int32, part.shape, 0) == lax.axis_index(TP)
    part = jnp.where(mine, part + own[None], part) * factor[...][None]
    sent[0] = part.astype(BF16)
    sent[1] = part.astype(BF16)


def combine(parts, sent, near, first):
    one = parts[0, 0].astype(F32)
    two = parts[1, 0].astype(F32)
    for device in range(1, parts.shape[1]):
        one = one + parts[0, device].astype(F32)
        two = two + parts[1, device].astype(F32)
    first[...] = one
    both = (one + two).astype(BF16)
    for device in range(sent.shape[0]):
        sent[device] = both
    for device in range(near.shape[0]):
        near[device] = both


def before(steps, first):
    total = jnp.where(lax.axis_index("core") == 1, first[...], 0.0)
    here = lax.axis_index(AXES[:2])
    for z in range(steps.shape[0]):
        total = total + jnp.where(z < here, steps[z].astype(F32), 0.0)
    return total


def judge(steps, first, start_latent, latents, sent):
    change = fold(start_latent[...] - latents[0]) + before(steps, first)
    count = change.size * lax.axis_size(TP)
    part = jnp.sum(change * change, axis=0, keepdims=True) / count
    sent[...] = jnp.broadcast_to(part, sent.shape)


def finish(parts, steps, first, start_latent, new_latents, step_error):
    half = LANES // 2
    change = before(steps, first)
    change = jnp.concatenate([change[:, :half], change[:, half:]], axis=0)
    new_latents[0] = start_latent[...] + change
    step_error[0] = jnp.sum(parts[...])


def local(latents, start_latent, t_index, dt_units, w_time, w_in, w_up, w_down, w_out):
    zs, devices = lax.axis_size(AXES[:2]), lax.axis_size(TP)
    tok_rows, channels = latents.shape[1:]
    width = w_in.shape[1]
    hid = w_up.shape[1]
    tokens = tok_rows * devices
    packed = jax.ShapeDtypeStruct((MODS_AT, LANES), F32)
    weights = (w_in, w_out.T, w_up, w_down)

    freqs, early = call(
        table,
        (
            jax.ShapeDtypeStruct((16, w_time.shape[0] // 2), F32),
            pltpu.SMEM((1,), jnp.int32),
        ),
        [],
        "table",
        flops=1 << 34,
        out_specs=(VMEM, SMEM),
    )()
    early = early[0] != 0
    flag = early.astype(jnp.int32).reshape(1)
    sent, factor = call(
        prepare,
        [jax.ShapeDtypeStruct((devices, 16, LANES), F32), packed],
        [SMEM] * 3 + [VMEM] * 3,
        "prepare",
        flops=1 << 34,
    )(t_index, dt_units, flag, freqs, latents, w_time.T)
    got = lax.all_to_all(sent, TP, 0, 0, tiled=True)
    sent = call(
        block,
        jax.ShapeDtypeStruct((2, devices, MODS_AT, LANES), BF16),
        [VMEM] * 6,
        "block",
        flops=2 * tokens * width * (hid + channels) + 2 * hid * width * channels,
        scratch=[
            pltpu.VMEM((tokens, width), F32),
            pltpu.VMEM((tokens, width), BF16),
        ],
        limit=32,
    )(got, factor, *weights)
    sent = sent.reshape(2 * devices, MODS_AT, LANES)
    parts = lax.all_to_all(sent, AXES[2:], 0, 0, tiled=True)
    parts = parts.reshape(2, devices, MODS_AT, LANES)
    sent, close, first = call(
        combine,
        [jax.ShapeDtypeStruct((n, MODS_AT, LANES), BF16) for n in (zs, NEAR)] + [packed],
        [VMEM],
        "combine",
    )(parts)

    def errors(steps, *shape):
        return call(
            judge,
            jax.ShapeDtypeStruct(shape + (LANES,), F32),
            [VMEM] * 4,
            "judge",
        )(steps, first, start_latent, latents)

    def ahead(close):
        return errors(lax.all_to_all(close, "near", 0, 0, tiled=True), MODS_AT)

    def gather(part):
        part = jnp.sum(lax.all_gather(part[:1], "x"), axis=0)
        return lax.all_gather(part, "y")

    def close_up(parts, steps):
        return call(
            finish,
            (jax.ShapeDtypeStruct(latents.shape, F32), jax.ShapeDtypeStruct((1,), F32)),
            [VMEM] * 4,
            "finish",
            out_specs=(VMEM, SMEM),
        )(parts, steps, first, start_latent)

    def exchange(parts, steps):
        totals = lax.all_to_all(errors(steps, devices, 1), TP, 0, 0, tiled=True)
        return close_up(totals, steps)

    part = lax.cond(early, ahead, lambda close: first, close)
    steps = lax.all_to_all(sent, AXES[:2], 0, 0, tiled=True)
    soon = lax.cond(early, gather, lambda part: part[: lax.axis_size("y"), None], part)
    new_latents, step_error = lax.cond(early, close_up, exchange, soon, steps)
    return (new_latents, step_error)


def solution(mesh):
    tm, tp = (mesh.shape["tm"], mesh.shape["tp"])
    side = math.isqrt(tp)
    grid = Mesh(mesh.devices.reshape(tm // 2 // NEAR, NEAR, 2, side, side), AXES)
    steps = AXES[:3]
    in_specs = (
        P(steps, TP, None),
        P(TP, None),
        P(steps),
        P(steps),
        P(None, TP),
        P(),
        P(None, TP),
        P(TP, None),
        P(),
    )
    out_specs = (P(steps, TP, None), P(steps))
    return jax.shard_map(local, mesh=grid, in_specs=in_specs, out_specs=out_specs, check_vma=False)
```

```python
import math

import jax
import jax.numpy as jnp
from jax import lax
from jax.experimental import pallas as pl
from jax.experimental.pallas import tpu as pltpu
from jax.sharding import Mesh
from jax.sharding import PartitionSpec as P

LANES = 128
MODS_AT = 8
NEAR = 4
AXES = ("far", "near", "core", "y", "x")
TP = AXES[3:]
SMEM = pl.BlockSpec(memory_space=pltpu.SMEM)
VMEM = pl.BlockSpec(memory_space=pltpu.VMEM)
F32 = jnp.float32
BF16 = jnp.bfloat16


def call(body, out_shape, in_specs, name, flops=0, scratch=(), limit=16, out_specs=None):
    return pl.pallas_call(
        body,
        out_shape=out_shape,
        in_specs=in_specs,
        out_specs=out_specs or jax.tree.map(lambda _: VMEM, out_shape),
        scratch_shapes=list(scratch),
        cost_estimate=pl.CostEstimate(flops=flops, bytes_accessed=1 << 20, transcendentals=0),
        compiler_params=pltpu.CompilerParams(vmem_limit_bytes=limit << 20),
        name=name,
    )


def fold(rows):
    half = rows.shape[0] // 2
    return jnp.concatenate([rows[:half], rows[half:]], axis=1)


def swap(value):
    return pltpu.roll(value, value.shape[-1] // 2, value.ndim - 1)


def left(shape):
    return lax.broadcasted_iota(jnp.int32, shape, len(shape) - 1) < shape[-1] // 2


def split(value):
    high = value.astype(BF16).astype(F32)
    return high, value - high


def table(freqs, early):
    early[0] = (lax.axis_index("far") == 0).astype(jnp.int32)
    half = freqs.shape[1]
    order = lax.broadcasted_iota(jnp.int32, freqs.shape, 1).astype(F32)
    freqs[...] = jnp.exp(-jnp.log(jnp.full(freqs.shape, 10000.0, F32)) * order / half)


def prepare(t_index, dt_units, flag, freqs, latents, w_time, sent, factor):
    angle = jnp.full(freqs.shape, t_index[0], jnp.int32).astype(F32) * freqs[...]
    emb = jnp.concatenate([jnp.cos(angle), jnp.sin(angle)], axis=1).astype(BF16)
    factor[...] = jnp.full(factor.shape, dt_units[0], jnp.int32).astype(F32) * 0.0078125
    lat = fold(latents[0])
    dims = (((1,), (1,)), ((), ()))
    mods = lax.dot_general(emb, w_time[...], dims, preferred_element_type=F32)[:1]
    gap = jnp.zeros((1, LANES // 2), F32)
    odd = lax.axis_index(TP) % 2 == 1
    mods = jnp.where(odd, jnp.concatenate([gap, mods], 1), jnp.concatenate([mods, gap], 1))
    lines = mods.shape[1] // LANES
    rows = [lat] + [mods[:, i * LANES : (i + 1) * LANES] for i in range(lines)]
    rows.append(jnp.zeros((16 - MODS_AT - lines, LANES), F32))
    block = jnp.concatenate(rows, axis=0)
    for device in range(sent.shape[0]):
        sent[device] = block


def block(got, factor, w_in, w_out_t, w_up, w_down, sent, hidden, normed):
    devices = got.shape[0]
    width = w_in.shape[1]
    count = width // LANES
    pairs = []
    for device in range(0, devices, 2):
        even = [got[device, MODS_AT + i : MODS_AT + i + 1, :] for i in range(5)]
        odd = [got[device + 1, MODS_AT + i : MODS_AT + i + 1, :] for i in range(5)]
        pairs += even[:4] + [even[4] + odd[0]] + odd[1:]
    shift, scale, gate = pairs[:count], pairs[count : 2 * count], pairs[2 * count :]
    dims = (((1,), (1,)), ((), ()))
    gated = w_out_t[...].astype(F32) * jnp.concatenate(gate, axis=1)
    high, low = split(gated)
    gated = jnp.concatenate([high, low], axis=0).astype(BF16)
    down = lax.dot_general(w_down[...], gated, dims, preferred_element_type=F32)
    down = down + swap(down)
    high, low = split(down)
    down = jnp.where(left(down.shape), high, low).astype(BF16)

    lat = got[:, :MODS_AT, :].reshape(devices * MODS_AT, LANES)
    lat = jnp.concatenate([lat[:, : LANES // 2], lat[:, LANES // 2 :]], axis=0).astype(BF16)
    tokens = lat.shape[0]
    step = 512
    columns = w_in[:, :LANES].astype(F32)
    for start in range(LANES, width, LANES):
        columns = columns + w_in[:, start : start + LANES].astype(F32)
    high, low = split(columns)
    rest, last = split(low)
    columns = jnp.concatenate([high, rest, last], axis=1).astype(BF16)
    total = jnp.dot(lat, columns, preferred_element_type=F32)
    total = total[:, :LANES] + (total[:, LANES : 2 * LANES] + total[:, 2 * LANES :])
    mean = jnp.sum(total, axis=1, keepdims=True) / width
    total = jnp.zeros((tokens, LANES), F32)
    for start in range(0, width, step):
        center = jnp.dot(lat, w_in[:, start : start + step], preferred_element_type=F32) - mean
        hidden[:, start : start + step] = center
        for at in range(0, step, LANES):
            total = total + center[:, at : at + LANES] * center[:, at : at + LANES]

    own = got[lax.axis_index(TP), :MODS_AT, :]
    own = jnp.concatenate([own[:, : LANES // 2], own[:, LANES // 2 :]], axis=0).astype(BF16)
    high, low = split(jnp.dot(own, w_in[...], preferred_element_type=F32))
    rest, last = split(low)
    own = jnp.concatenate([high, rest, last], axis=0).astype(BF16)
    own = lax.dot_general(own, w_out_t[...], dims, preferred_element_type=F32)
    own = fold(own[:16] + own[16:32] + own[32:48])
    spread = jnp.sum(total, axis=1, keepdims=True) / width
    inverse = 1.0 / jnp.sqrt(spread + 1e-06)
    for i in range(count):
        at = slice(i * LANES, (i + 1) * LANES)
        value = hidden[:, at] * inverse * (1.0 + scale[i]) + shift[i]
        normed[:, at] = value.astype(BF16)
    up = jnp.dot(normed[...], w_up[...], preferred_element_type=F32)
    act = jax.nn.gelu(up, approximate=True).astype(BF16)
    part = jnp.dot(act, down, preferred_element_type=F32)
    part = part + swap(part)
    half = tokens // 2
    part = jnp.where(left((half, LANES)), part[:half], part[half:])
    part = part.reshape(devices, MODS_AT, LANES)
    mine = lax.broadcasted_iota(jnp.int32, part.shape, 0) == lax.axis_index(TP)
    part = jnp.where(mine, part + own[None], part) * factor[...][None]
    sent[0] = part.astype(BF16)
    sent[1] = part.astype(BF16)


def combine(parts, sent, near, first):
    one = parts[0, 0].astype(F32)
    two = parts[1, 0].astype(F32)
    for device in range(1, parts.shape[1]):
        one = one + parts[0, device].astype(F32)
        two = two + parts[1, device].astype(F32)
    first[...] = one
    both = (one + two).astype(BF16)
    for device in range(sent.shape[0]):
        sent[device] = both
    for device in range(near.shape[0]):
        near[device] = both


def before(steps, first):
    total = jnp.where(lax.axis_index("core") == 1, first[...], 0.0)
    here = lax.axis_index(AXES[:2])
    for z in range(steps.shape[0]):
        total = total + jnp.where(z < here, steps[z].astype(F32), 0.0)
    return total


def judge(steps, first, start_latent, latents, sent, rows):
    half = LANES // 2
    change = before(steps, first)
    rows[...] = start_latent[...] + jnp.concatenate([change[:, :half], change[:, half:]], axis=0)
    change = fold(start_latent[...] - latents[0]) + change
    count = change.size * lax.axis_size(TP)
    part = jnp.sum(change * change, axis=0, keepdims=True) / count
    sent[...] = jnp.broadcast_to(part, sent.shape)


def finish(parts, rows, new_latents, step_error):
    new_latents[0] = rows[...]
    step_error[0] = jnp.sum(parts[...])


def local(latents, start_latent, t_index, dt_units, w_time, w_in, w_up, w_down, w_out):
    zs, devices = lax.axis_size(AXES[:2]), lax.axis_size(TP)
    tok_rows, channels = latents.shape[1:]
    width = w_in.shape[1]
    hid = w_up.shape[1]
    tokens = tok_rows * devices
    packed = jax.ShapeDtypeStruct((MODS_AT, LANES), F32)
    weights = (w_in, w_out.T, w_up, w_down)

    freqs, early = call(
        table,
        (
            jax.ShapeDtypeStruct((16, w_time.shape[0] // 2), F32),
            pltpu.SMEM((1,), jnp.int32),
        ),
        [],
        "table",
        flops=1 << 34,
        out_specs=(VMEM, SMEM),
    )()
    early = early[0] != 0
    flag = early.astype(jnp.int32).reshape(1)
    sent, factor = call(
        prepare,
        [jax.ShapeDtypeStruct((devices, 16, LANES), F32), packed],
        [SMEM] * 3 + [VMEM] * 3,
        "prepare",
        flops=1 << 34,
    )(t_index, dt_units, flag, freqs, latents, w_time.T)
    got = lax.all_to_all(sent, TP, 0, 0, tiled=True)
    sent = call(
        block,
        jax.ShapeDtypeStruct((2, devices, MODS_AT, LANES), BF16),
        [VMEM] * 6,
        "block",
        flops=2 * tokens * width * (hid + channels) + 2 * hid * width * channels,
        scratch=[
            pltpu.VMEM((tokens, width), F32),
            pltpu.VMEM((tokens, width), BF16),
        ],
        limit=32,
    )(got, factor, *weights)
    sent = sent.reshape(2 * devices, MODS_AT, LANES)
    parts = lax.all_to_all(sent, AXES[2:], 0, 0, tiled=True)
    parts = parts.reshape(2, devices, MODS_AT, LANES)
    sent, close, first = call(
        combine,
        [jax.ShapeDtypeStruct((n, MODS_AT, LANES), BF16) for n in (zs, NEAR)] + [packed],
        [VMEM],
        "combine",
    )(parts)

    def errors(steps, *shape):
        rows = jax.ShapeDtypeStruct((tok_rows, channels), F32)
        return call(
            judge,
            [jax.ShapeDtypeStruct(shape + (LANES,), F32), rows],
            [VMEM] * 4,
            "judge",
        )(steps, first, start_latent, latents)

    def ahead(close):
        return tuple(errors(lax.all_to_all(close, "near", 0, 0, tiled=True), MODS_AT))

    def gather(part):
        part = jnp.sum(lax.all_gather(part[:1], "x"), axis=0)
        return lax.all_gather(part, "y")

    def close_up(parts, rows):
        return call(
            finish,
            (jax.ShapeDtypeStruct(latents.shape, F32), jax.ShapeDtypeStruct((1,), F32)),
            [VMEM] * 2,
            "finish",
            out_specs=(VMEM, SMEM),
        )(parts, rows)

    def exchange(parts, rows, steps):
        parts, rows = errors(steps, devices, 1)
        return close_up(lax.all_to_all(parts, TP, 0, 0, tiled=True), rows)

    part, rows = lax.cond(early, ahead, lambda close: (first, start_latent), close)
    steps = lax.all_to_all(sent, AXES[:2], 0, 0, tiled=True)
    soon = lax.cond(early, gather, lambda part: part[: lax.axis_size("y"), None], part)
    new_latents, step_error = lax.cond(
        early, lambda parts, rows, steps: close_up(parts, rows), exchange, soon, rows, steps
    )
    return (new_latents, step_error)


def solution(mesh):
    tm, tp = (mesh.shape["tm"], mesh.shape["tp"])
    side = math.isqrt(tp)
    grid = Mesh(mesh.devices.reshape(tm // 2 // NEAR, NEAR, 2, side, side), AXES)
    steps = AXES[:3]
    in_specs = (
        P(steps, TP, None),
        P(TP, None),
        P(steps),
        P(steps),
        P(None, TP),
        P(),
        P(None, TP),
        P(TP, None),
        P(),
    )
    out_specs = (P(steps, TP, None), P(steps))
    return jax.shard_map(local, mesh=grid, in_specs=in_specs, out_specs=out_specs, check_vma=False)
```

```python
import math

import jax
import jax.numpy as jnp
from jax import lax
from jax.experimental import pallas as pl
from jax.experimental.pallas import tpu as pltpu
from jax.sharding import Mesh
from jax.sharding import PartitionSpec as P

LANES = 128
MODS_AT = 8
NEAR = 4
AXES = ("far", "near", "core", "y", "x")
TP = AXES[3:]
SMEM = pl.BlockSpec(memory_space=pltpu.SMEM)
VMEM = pl.BlockSpec(memory_space=pltpu.VMEM)
F32 = jnp.float32
BF16 = jnp.bfloat16


def call(body, out_shape, in_specs, name, flops=0, scratch=(), limit=16, out_specs=None):
    return pl.pallas_call(
        body,
        out_shape=out_shape,
        in_specs=in_specs,
        out_specs=out_specs or jax.tree.map(lambda _: VMEM, out_shape),
        scratch_shapes=list(scratch),
        cost_estimate=pl.CostEstimate(flops=flops, bytes_accessed=1 << 20, transcendentals=0),
        compiler_params=pltpu.CompilerParams(vmem_limit_bytes=limit << 20),
        name=name,
    )


def fold(rows):
    half = rows.shape[0] // 2
    return jnp.concatenate([rows[:half], rows[half:]], axis=1)


def swap(value):
    return pltpu.roll(value, value.shape[-1] // 2, value.ndim - 1)


def left(shape):
    return lax.broadcasted_iota(jnp.int32, shape, len(shape) - 1) < shape[-1] // 2


def split(value):
    high = value.astype(BF16).astype(F32)
    return high, value - high


def table(freqs):
    half = freqs.shape[1]
    order = lax.broadcasted_iota(jnp.int32, freqs.shape, 1).astype(F32)
    freqs[...] = jnp.exp(-jnp.log(jnp.full(freqs.shape, 10000.0, F32)) * order / half)


def prepare(t_index, dt_units, flag, freqs, latents, w_time, sent, factor):
    angle = jnp.full(freqs.shape, t_index[0], jnp.int32).astype(F32) * freqs[...]
    emb = jnp.concatenate([jnp.cos(angle), jnp.sin(angle)], axis=1).astype(BF16)
    factor[...] = jnp.full(factor.shape, dt_units[0], jnp.int32).astype(F32) * 0.0078125
    lat = fold(latents[0])
    dims = (((1,), (1,)), ((), ()))
    mods = lax.dot_general(emb, w_time[...], dims, preferred_element_type=F32)[:1]
    gap = jnp.zeros((1, LANES // 2), F32)
    odd = lax.axis_index(TP) % 2 == 1
    mods = jnp.where(odd, jnp.concatenate([gap, mods], 1), jnp.concatenate([mods, gap], 1))
    lines = mods.shape[1] // LANES
    rows = [lat] + [mods[:, i * LANES : (i + 1) * LANES] for i in range(lines)]
    rows.append(jnp.zeros((16 - MODS_AT - lines, LANES), F32))
    block = jnp.concatenate(rows, axis=0)
    for device in range(sent.shape[0]):
        sent[device] = block


def block(got, factor, w_in, w_out_t, w_up, w_down, sent, hidden, normed):
    devices = got.shape[0]
    width = w_in.shape[1]
    count = width // LANES
    pairs = []
    for device in range(0, devices, 2):
        even = [got[device, MODS_AT + i : MODS_AT + i + 1, :] for i in range(5)]
        odd = [got[device + 1, MODS_AT + i : MODS_AT + i + 1, :] for i in range(5)]
        pairs += even[:4] + [even[4] + odd[0]] + odd[1:]
    shift, scale, gate = pairs[:count], pairs[count : 2 * count], pairs[2 * count :]
    dims = (((1,), (1,)), ((), ()))
    lat = got[:, :MODS_AT, :].reshape(devices * MODS_AT, LANES)
    lat = jnp.concatenate([lat[:, : LANES // 2], lat[:, LANES // 2 :]], axis=0).astype(BF16)
    tokens = lat.shape[0]
    step = 512
    columns = w_in[:, :LANES].astype(F32)
    for start in range(LANES, width, LANES):
        columns = columns + w_in[:, start : start + LANES].astype(F32)
    high, low = split(columns)
    rest, last = split(low)
    columns = jnp.concatenate([high, rest, last], axis=1).astype(BF16)
    total = jnp.dot(lat, columns, preferred_element_type=F32)
    total = total[:, :LANES] + (total[:, LANES : 2 * LANES] + total[:, 2 * LANES :])
    mean = jnp.sum(total, axis=1, keepdims=True) / width
    total = jnp.zeros((tokens, LANES), F32)
    for start in range(0, width, step):
        center = jnp.dot(lat, w_in[:, start : start + step], preferred_element_type=F32) - mean
        hidden[:, start : start + step] = center
        for at in range(0, step, LANES):
            total = total + center[:, at : at + LANES] * center[:, at : at + LANES]

    own = got[lax.axis_index(TP), :MODS_AT, :]
    own = jnp.concatenate([own[:, : LANES // 2], own[:, LANES // 2 :]], axis=0).astype(BF16)
    high, low = split(jnp.dot(own, w_in[...], preferred_element_type=F32))
    rest, last = split(low)
    own = jnp.concatenate([high, rest, last], axis=0).astype(BF16)
    own = lax.dot_general(own, w_out_t[...], dims, preferred_element_type=F32)
    own = fold(own[:16] + own[16:32] + own[32:48])
    gated = w_out_t[...].astype(F32) * jnp.concatenate(gate, axis=1)
    high, low = split(gated)
    gated = jnp.concatenate([high, low], axis=0).astype(BF16)
    down = lax.dot_general(w_down[...], gated, dims, preferred_element_type=F32)
    down = down + swap(down)
    high, low = split(down)
    down = jnp.where(left(down.shape), high, low).astype(BF16)
    spread = jnp.sum(total, axis=1, keepdims=True) / width
    inverse = 1.0 / jnp.sqrt(spread + 1e-06)
    for i in range(count):
        at = slice(i * LANES, (i + 1) * LANES)
        value = hidden[:, at] * inverse * (1.0 + scale[i]) + shift[i]
        normed[:, at] = value.astype(BF16)
    up = jnp.dot(normed[...], w_up[...], preferred_element_type=F32)
    act = jax.nn.gelu(up, approximate=True).astype(BF16)
    part = jnp.dot(act, down, preferred_element_type=F32)
    part = part + swap(part)
    half = tokens // 2
    part = jnp.where(left((half, LANES)), part[:half], part[half:])
    part = part.reshape(devices, MODS_AT, LANES)
    mine = lax.broadcasted_iota(jnp.int32, part.shape, 0) == lax.axis_index(TP)
    part = jnp.where(mine, part + own[None], part) * factor[...][None]
    sent[0] = part.astype(BF16)
    sent[1] = part.astype(BF16)


def combine(parts, sent, near, first):
    one = parts[0, 0].astype(F32)
    two = parts[1, 0].astype(F32)
    for device in range(1, parts.shape[1]):
        one = one + parts[0, device].astype(F32)
        two = two + parts[1, device].astype(F32)
    first[...] = one
    both = (one + two).astype(BF16)
    for device in range(sent.shape[0]):
        sent[device] = both
    for device in range(near.shape[0]):
        near[device] = both


def before(steps, first):
    total = jnp.where(lax.axis_index("core") == 1, first[...], 0.0)
    here = lax.axis_index(AXES[:2])
    for z in range(steps.shape[0]):
        total = total + jnp.where(z < here, steps[z].astype(F32), 0.0)
    return total


def judge(steps, first, start_latent, latents, sent):
    change = fold(start_latent[...] - latents[0]) + before(steps, first)
    count = change.size * lax.axis_size(TP)
    part = jnp.sum(change * change, axis=0, keepdims=True) / count
    sent[...] = jnp.broadcast_to(part, sent.shape)


def finish(parts, steps, first, start_latent, new_latents, step_error):
    half = LANES // 2
    change = before(steps, first)
    change = jnp.concatenate([change[:, :half], change[:, half:]], axis=0)
    new_latents[0] = start_latent[...] + change
    step_error[0] = jnp.sum(parts[...])


def local(latents, start_latent, t_index, dt_units, w_time, w_in, w_up, w_down, w_out):
    zs, devices = lax.axis_size(AXES[:2]), lax.axis_size(TP)
    tok_rows, channels = latents.shape[1:]
    width = w_in.shape[1]
    hid = w_up.shape[1]
    tokens = tok_rows * devices
    packed = jax.ShapeDtypeStruct((MODS_AT, LANES), F32)
    weights = (w_in, w_out.T, w_up, w_down)

    early = lax.axis_index("far") == 0
    flag = early.astype(jnp.int32).reshape(1)
    freqs = call(
        table,
        jax.ShapeDtypeStruct((16, w_time.shape[0] // 2), F32),
        [],
        "table",
        flops=1 << 34,
    )()
    sent, factor = call(
        prepare,
        [jax.ShapeDtypeStruct((devices, 16, LANES), F32), packed],
        [SMEM] * 3 + [VMEM] * 3,
        "prepare",
        flops=1 << 34,
    )(t_index, dt_units, flag, freqs, latents, w_time.T)
    got = lax.all_to_all(sent, TP, 0, 0, tiled=True)
    sent = call(
        block,
        jax.ShapeDtypeStruct((2, devices, MODS_AT, LANES), BF16),
        [VMEM] * 6,
        "block",
        flops=2 * tokens * width * (hid + channels) + 2 * hid * width * channels,
        scratch=[
            pltpu.VMEM((tokens, width), F32),
            pltpu.VMEM((tokens, width), BF16),
        ],
        limit=32,
    )(got, factor, *weights)
    sent = sent.reshape(2 * devices, MODS_AT, LANES)
    parts = lax.all_to_all(sent, AXES[2:], 0, 0, tiled=True)
    parts = parts.reshape(2, devices, MODS_AT, LANES)
    sent, close, first = call(
        combine,
        [jax.ShapeDtypeStruct((n, MODS_AT, LANES), BF16) for n in (zs, NEAR)] + [packed],
        [VMEM],
        "combine",
    )(parts)

    def errors(steps, *shape):
        return call(
            judge,
            jax.ShapeDtypeStruct(shape + (LANES,), F32),
            [VMEM] * 4,
            "judge",
        )(steps, first, start_latent, latents)

    def ahead(close):
        return errors(lax.all_to_all(close, "near", 0, 0, tiled=True), MODS_AT)

    def gather(part):
        part = jnp.sum(lax.all_gather(part[:1], "x"), axis=0)
        return lax.all_gather(part, "y")

    def close_up(parts, steps):
        return call(
            finish,
            (jax.ShapeDtypeStruct(latents.shape, F32), jax.ShapeDtypeStruct((1,), F32)),
            [VMEM] * 4,
            "finish",
            out_specs=(VMEM, SMEM),
        )(parts, steps, first, start_latent)

    def exchange(parts, steps):
        totals = lax.all_to_all(errors(steps, devices, 1), TP, 0, 0, tiled=True)
        return close_up(totals, steps)

    part = lax.cond(early, ahead, lambda close: first, close)
    steps = lax.all_to_all(sent, AXES[:2], 0, 0, tiled=True)
    soon = lax.cond(early, gather, lambda part: part[: lax.axis_size("y"), None], part)
    new_latents, step_error = lax.cond(early, close_up, exchange, soon, steps)
    return (new_latents, step_error)


def solution(mesh):
    tm, tp = (mesh.shape["tm"], mesh.shape["tp"])
    side = math.isqrt(tp)
    grid = Mesh(mesh.devices.reshape(tm // 2 // NEAR, NEAR, 2, side, side), AXES)
    steps = AXES[:3]
    in_specs = (
        P(steps, TP, None),
        P(TP, None),
        P(steps),
        P(steps),
        P(None, TP),
        P(),
        P(None, TP),
        P(TP, None),
        P(),
    )
    out_specs = (P(steps, TP, None), P(steps))
    return jax.shard_map(local, mesh=grid, in_specs=in_specs, out_specs=out_specs, check_vma=False)
```
